128 devices in a mesh: dp: 2 (over core), context: 16 (over x, z), tensor: 4 (over y).
Axes of the slice: x: 4, y: 4, z: 4, core: 2. Of those that a mesh axis runs over, the one named last changes fastest.
Arguments:
- token_ids: int32 [24576], P(('dp', 'context')), parts along dimension 0, may hold values from 0 to 511
- subst_pos: int32 [1536], P(('dp', 'context')), parts along dimension 0, may hold values from 0 to 767, as said below
- subst_base: int32 [1536], P(('dp', 'context')), parts along dimension 0, may hold values from 0 to 511
- window_lengths: int32 [64], P('dp'), parts along dimension 0, may hold values from 1 to 768, 12288 in all
- embed_table: bfloat16 [512, 4096], replicated, may hold values from -6 to 6
- norm_gain: float32 [4096], replicated, may hold values from 0.5 to 1.5
- in_weight: bfloat16 [4096, 3, 4096], P('context', None, 'tensor'), may hold values from -0.09375 to 0.09375
- short_filter: float32 [3, 3, 4096], P(None, None, 'tensor'), may hold values from -4 to 4
- mr_filter: float32 [128, 4096], P(None, 'tensor'), may hold values from -0.5 to 0.5
- mr_decay: float32 [4096], P('tensor'), may hold values from 0.002 to 0.08
- out_weight: bfloat16 [4096, 4096], P('context', 'tensor'), may hold values from -0.09375 to 0.09375
Outputs:
- block_out: bfloat16 [24576, 4096], P(('dp', 'context'), 'tensor'), parts along dimension 0
The draws below stay inside these ranges and needn't reach their ends.
There are 2 independent parts, one for each index of `dp`. The reference program is written for one: setup_inputs(seed, part) draws one part's arguments, and reference() takes and returns one part's arrays. A program takes and returns all parts, laid end to end along the dimension named above; an argument that names none is the same for every part. Nothing has to cross between parts.
Inputs may be any that keep to these rules, and one draw needn't show every extreme that they name: `subst_pos`: the j-th substitution of a shard lies in that shard's rows j * 16 to (j + 1) * 16 - 1; each shard's first substitution is at row 0 and its last at row 767. `window_lengths`: the lengths sum to 12288.
All inputs are finite; a program needn't handle non-finite values.
Results may differ from the reference program's by a relative error of at most 0.0085.
Values may be sent and summed in bfloat16 or wider, within the bound.
A program may use at most 320 MiB of HBM per device.

```python
import math
import jax
import jax.numpy as jnp
import numpy as np
from jax import lax

D = 4096
VOCAB = 512
LH = 128
STRIDE = 16
TOK_DEV = 768
TOKENS = 12288
SUBS = 768
NDOC = 32


def draw_subst_pos(key, part):
    key = jax.random.fold_in(key, 7)
    shards = TOKENS // TOK_DEV
    per_shard = TOK_DEV // STRIDE
    offsets = jax.random.randint(key, (shards, per_shard), 0, STRIDE, dtype=jnp.int32)
    row_base = jnp.arange(per_shard, dtype=jnp.int32) * STRIDE
    position = row_base[None, :] + offsets
    position = position.at[:, 0].set(0).at[:, per_shard - 1].set(TOK_DEV - 1)
    return position.reshape(-1).astype(jnp.int32)


def plant(values, rng, low, largest):
    shape = values.shape
    index_at = [jax.random.randint(jax.random.fold_in(rng, axis), (), 0, shape[axis]) for axis in range(len(shape))]
    values = values.at[tuple(index_at)].set(low)
    longest = shape.index(max(shape))
    index_at[longest] = (index_at[longest] + 1) % shape[longest]
    return values.at[tuple(index_at)].set(largest)


def shard_levels(key, dims, cuts, smallest, top_value):
    factor_of, own = 1.0, jax.random.fold_in(key, 6)
    for dim, parts in cuts:
        heights = jnp.exp(jax.random.uniform(jax.random.fold_in(own, dim), (parts,), jnp.float32, smallest / len(cuts), top_value / len(cuts)))
        factor_of = factor_of * jnp.repeat(heights, dims[dim] // parts).reshape([-1 if axis == dim else 1 for axis in range(len(dims))])
    return factor_of


def cumulative_ranks(number_of, slope):
    portions = [(1 << 20) // math.isqrt(grade ** slope) + 1 for grade in range(1, number_of + 1)]
    spread = 1 + sum(portions) // (1 << 30)
    return np.cumsum(np.array([max(1, weight // spread) for weight in portions]))


def ranked(key, shape, count, slope):
    listing = cumulative_ranks(count, slope)
    pick = jax.random.randint(jax.random.fold_in(key, 1), shape, 0, int(listing[count - 1]))
    rank = jnp.searchsorted(jnp.asarray(listing, jnp.int32), pick, side="right")
    return jax.random.permutation(jax.random.fold_in(key, 2), count)[rank].astype(jnp.int32)


def profile(amount, total, limit, skew):
    loads = [(1 << 20) // math.isqrt(grade ** skew) + 1 for grade in range(2, amount + 1)]
    spare, counts = total - limit - (amount - 1), [1] * (amount - 1)
    while spare > 0:
        free = [i for i in range(amount - 1) if counts[i] < limit]
        pool, remaining = sum([loads[i] for i in free]), spare
        for i in free:
            addition = min(limit - counts[i], max(1, remaining * loads[i] // pool), spare)
            counts[i] = counts[i] + addition
            spare = spare - addition
    return np.array([limit] + counts)


def ragged(stream_key, number_of, total, reach, lean):
    if number_of == 2:
        one = jax.random.randint(stream_key, (), max(1, total - reach), min(reach, total - 1) + 1)
        return jnp.stack([one, total - one])
    tallies = jnp.asarray(profile(number_of, total, reach, lean), jnp.int32)
    twos = (number_of - 1) // 2
    source_of, taker = tallies[1:1 + 2 * twos:2], tallies[2:2 + 2 * twos:2]
    margin = jnp.minimum(source_of - 1, reach - taker)
    moved = jax.random.randint(jax.random.fold_in(stream_key, 1), (twos,), 0, 1 << 20) % (margin + 1)
    tallies = tallies.at[1:1 + 2 * twos:2].set(source_of - moved).at[2:2 + 2 * twos:2].set(taker + moved)
    return tallies[jax.random.permutation(jax.random.fold_in(stream_key, 2), number_of)]


def gaussian(key, extent, width, reach, cuts=(), kind=jnp.bfloat16):
    loudness = shard_levels(key, extent, cuts, -0.22, 0.18) if cuts else 1.0
    values = jax.random.normal(key, extent, jnp.float32) * width * loudness
    return jnp.minimum(jnp.maximum(values, -reach), reach).astype(kind)


def setup_inputs(seed: int = 0, part: int = 0) -> dict:
    key_of = jax.random.split(jax.random.key(seed), 12)
    own_keys = jax.random.split(jax.random.fold_in(key_of[11], part), 12)
    token_ids = plant(ranked(own_keys[0], (TOKENS,), VOCAB, 2), jax.random.fold_in(own_keys[0], 3), 0, VOCAB - 1).astype(jnp.int32)
    subst_pos = draw_subst_pos(jax.random.fold_in(jax.random.fold_in(key_of[11], part), 71), part)
    subst_base = plant(jax.random.randint(own_keys[2], (SUBS,), 0, VOCAB), jax.random.fold_in(own_keys[2], 1), 0, VOCAB - 1).astype(jnp.int32)
    window_lengths = ragged(own_keys[3], NDOC, TOKENS, TOK_DEV, 2).astype(jnp.int32)
    embed_table = gaussian(key_of[4], (VOCAB, D), 1.0, 6.0)
    norm_gain = jnp.clip(1.0 + 0.1 * jax.random.normal(key_of[5], (D,), jnp.float32), 0.5, 1.5)
    in_weight = gaussian(key_of[6], (D, 3, D), D ** -0.5, 0.09375, ((0, 16), (2, 4)))
    short_filter = gaussian(key_of[7], (3, 3, D), 0.6, 4.0, ((2, 4),), jnp.float32)
    mr_filter = gaussian(key_of[8], (LH, D), 0.09, 0.5, ((1, 4),), jnp.float32)
    mr_decay = jnp.clip(jnp.exp(math.log(0.08) - 3.6888794 * jax.random.uniform(key_of[9], (D,), jnp.float32) ** shard_levels(key_of[9], (D,), ((0, 4),), -0.2, 0.2)), 0.002, 0.08)
    out_weight = gaussian(key_of[10], (D, D), D ** -0.5, 0.09375, ((0, 16), (1, 4)))
    return {"token_ids": token_ids, "subst_pos": subst_pos, "subst_base": subst_base, "window_lengths": window_lengths, "embed_table": embed_table, "norm_gain": norm_gain, "in_weight": in_weight, "short_filter": short_filter, "mr_filter": mr_filter, "mr_decay": mr_decay, "out_weight": out_weight}


def window_age(window_lengths, first_row, row_count):
    starts = (jnp.cumsum(window_lengths) - window_lengths).astype(jnp.int32)
    positions = first_row + jnp.arange(row_count, dtype=jnp.int32)
    matches = starts[None, :] <= positions[:, None]
    doc_begin = lax.optimization_barrier(jnp.max(jnp.where(matches, starts[None, :], -1), axis=1)).astype(jnp.int32)
    return jnp.where(doc_begin >= 0, positions - doc_begin, -1).astype(jnp.int32)

def short_mix(extended, filters, row_age):
    out_rows = extended.shape[0] - 2
    result = jnp.zeros((out_rows,) + extended.shape[1:], jnp.float32)
    for tap_index in range(3):
        keep = (tap_index <= row_age).astype(jnp.float32)[:, None, None]
        window = extended[2 - tap_index:2 - tap_index + out_rows].astype(jnp.float32)
        result = result + filters[tap_index][None] * window * keep
    return result

def reference(token_ids, subst_pos, subst_base, window_lengths, embed_table, norm_gain, in_weight, short_filter, mr_filter, mr_decay, out_weight):
    shards = TOKENS // TOK_DEV
    shard_base = (jnp.arange(shards, dtype=jnp.int32) * TOK_DEV)[:, None]
    global_pos = (subst_pos.reshape(shards, -1) + shard_base).reshape(-1).astype(jnp.int32)
    new_ids = token_ids.at[global_pos].set(subst_base)
    embedded = jnp.take(embed_table, new_ids, axis=0)
    x_wide = embedded.astype(jnp.float32)
    scale = lax.rsqrt(lax.optimization_barrier(jnp.mean(x_wide * x_wide, axis=1, keepdims=True)) + 1e-06)
    normed = (x_wide * scale * norm_gain[None, :]).astype(jnp.bfloat16)
    projected_in = jnp.dot(normed, in_weight.reshape(D, 3 * D), preferred_element_type=jnp.float32)
    projected_in = projected_in.astype(jnp.bfloat16).reshape(TOKENS, 3, D)
    row_age = window_age(window_lengths, jnp.int32(0), TOKENS)
    padded = jnp.concatenate([jnp.zeros((2, 3, D), jnp.bfloat16), projected_in], axis=0)
    short_out = short_mix(padded, short_filter, row_age)
    product = (short_out[:, 1, :] * short_out[:, 2, :]).astype(jnp.bfloat16)
    tap_table = mr_filter * jnp.exp(-mr_decay[None, :] * jnp.arange(LH, dtype=jnp.float32)[:, None])
    product_pad = jnp.concatenate([jnp.zeros((LH - 1, D), jnp.bfloat16), product], axis=0)

    def add_tap(tap_index, running):
        window = lax.dynamic_slice_in_dim(product_pad, (LH - 1 - tap_index).astype(jnp.int32), TOKENS, 0).astype(jnp.float32)
        keep = (tap_index <= row_age).astype(jnp.float32)[:, None]
        coeff = lax.dynamic_slice_in_dim(tap_table, tap_index.astype(jnp.int32), 1, 0)
        return running + coeff * window * keep
    long_out = lax.fori_loop(jnp.int32(0), jnp.int32(LH), add_tap, jnp.zeros((TOKENS, D), jnp.float32))
    gated_out = (short_out[:, 0, :] * long_out).astype(jnp.bfloat16)
    projected = jnp.dot(gated_out, out_weight, preferred_element_type=jnp.float32)
    return (x_wide + projected).astype(jnp.bfloat16)
```

```python
import functools

import jax
import jax.numpy as jnp
from jax import lax
from jax.experimental import pallas as pl
from jax.experimental.pallas import tpu as pltpu
from jax.sharding import PartitionSpec as P

ROWS = 768
HALO = 144
EXT = HALO + ROWS
TAPS = 128
CB = 256
LANES = 128
R = 32
GROUP = 4
MAX_PAIRS = ROWS // R + 32


def passed_along(value, axis, steps):
    count = lax.axis_size(axis)
    first, last = (max(0, -steps), min(count, count - steps))
    return lax.ppermute(value, axis, [(source, source + steps) for source in range(first, last)])


def conv_kernel(
    begin_ref,
    end_ref,
    ids_ref,
    age_ref,
    tab_ref,
    short_ref,
    filt_ref,
    decay_ref,
    out_ref,
    onehot,
    mask1,
    mask2,
    src,
    prod,
    window,
    taps,
    longs,
    pair_row,
    pair_begin,
    pair_end,
    pair_count,
):
    windows = begin_ref.shape[0]

    @pl.when(pl.program_id(0) == 0)
    def _():
        vocab = onehot.shape[1]
        ids = jnp.broadcast_to(ids_ref[...], (EXT, vocab))
        onehot[...] = jnp.where(ids == lax.broadcasted_iota(jnp.int32, (EXT, vocab), 1), 1.0, 0.0).astype(jnp.bfloat16)
        age = jnp.broadcast_to(age_ref[...], (EXT, LANES))
        mask1[...] = (age >= 1).astype(jnp.float32)
        mask2[...] = (age >= 2).astype(jnp.float32)
        src[:, 0:8, :] = jnp.zeros((3, 8, CB), jnp.float32)

        def per_window(w, count):
            low = jnp.maximum(begin_ref[w], HALO)
            high = jnp.minimum(end_ref[w], EXT)
            first = (low - HALO) // R
            last = jnp.where(high > low, (high - 1 - HALO) // R + 1, first)

            def per_piece(piece, k):
                pair_row[k] = HALO + piece * R
                pair_begin[k] = begin_ref[w]
                pair_end[k] = end_ref[w]
                return k + 1

            return lax.fori_loop(first, last, per_piece, count)

        pair_count[0] = lax.fori_loop(0, windows, per_window, 0)

    for g in range(3):
        table = tab_ref[:, g].reshape(CB, tab_ref.shape[3])
        src[g, 8:, :] = lax.dot_general(
            onehot[...], table, (((1,), (1,)), ((), ())), preferred_element_type=jnp.float32
        )
    tap_index = lax.broadcasted_iota(jnp.int32, (TAPS, CB), 0).astype(jnp.float32)
    taps[...] = filt_ref[...] * jnp.exp(-decay_ref[...] * tap_index)

    def mixed(g, low, count, lanes):
        return (
            short_ref[0, g : g + 1, lanes] * src[g, pl.ds(8 + low, count), lanes]
            + short_ref[1, g : g + 1, lanes] * (src[g, pl.ds(7 + low, count), lanes] * mask1[pl.ds(low, count), :])
            + short_ref[2, g : g + 1, lanes] * (src[g, pl.ds(6 + low, count), lanes] * mask2[pl.ds(low, count), :])
        )

    tiles = [slice(at, at + LANES) for at in range(0, CB, LANES)]
    for lanes in tiles:
        for low in range(0, EXT, 48):
            product = mixed(1, low, 48, lanes) * mixed(2, low, 48, lanes)
            prod[pl.ds(low, 48), lanes] = product.astype(jnp.bfloat16).astype(jnp.float32)

    def per_pair(k, carry):
        row = pl.multiple_of(pair_row[k], 16)
        begin = pair_begin[k]
        end = pair_end[k]
        at = row - TAPS + lax.broadcasted_iota(jnp.int32, (TAPS + R, LANES), 0)
        inside = (at >= begin) & (at < end)
        mine = inside[TAPS:]
        for lanes in tiles:
            window[...] = jnp.where(inside, prod[pl.ds(row - TAPS, TAPS + R), lanes], 0.0)
            sums = [jnp.zeros((8, LANES), jnp.float32) for _ in range(R // 8)]
            for phase in range(8):
                for block in range(0, TAPS // 8, GROUP):
                    held = [
                        jnp.broadcast_to(taps[pl.ds(phase + 8 * (block + m), 1), lanes], (8, LANES))
                        for m in range(GROUP)
                    ]
                    views = {
                        q: window[pl.ds(TAPS + 8 * q - phase, 8), :]
                        for q in range(-(block + GROUP - 1), R // 8 - block)
                    }
                    for i in range(R // 8):
                        for m in range(GROUP):
                            sums[i] = sums[i] + held[m] * views[i - block - m]
            result = jnp.concatenate(sums, axis=0)
            where = pl.ds(pl.multiple_of(row - HALO, 16), R)
            longs[where, lanes] = jnp.where(mine, result, longs[where, lanes])
        return carry

    lax.fori_loop(0, pair_count[0], per_pair, 0)
    for lanes in tiles:
        for low in range(0, ROWS, 48):
            gated = mixed(0, HALO + low, 48, lanes) * longs[pl.ds(low, 48), lanes]
            out_ref[pl.ds(low, 48), lanes] = gated.astype(jnp.bfloat16)


def gated_rows(begin, end, ids, age, table, short_filter, mr_filter, mr_decay, first, count):
    vocab = table.shape[3]
    steps = count // CB
    offset = first // CB
    smem = pl.BlockSpec(memory_space=pltpu.SMEM)
    return pl.pallas_call(
        conv_kernel,
        grid=(steps,),
        out_shape=jax.ShapeDtypeStruct((ROWS, count), jnp.bfloat16),
        in_specs=[
            smem,
            smem,
            pl.BlockSpec((EXT, 1), lambda i: (0, 0)),
            pl.BlockSpec((EXT, 1), lambda i: (0, 0)),
            pl.BlockSpec((CB // 32, 3, 32, vocab), lambda i: (i + offset, 0, 0, 0)),
            pl.BlockSpec((3, 3, CB), lambda i: (0, 0, i + offset)),
            pl.BlockSpec((TAPS, CB), lambda i: (0, i + offset)),
            pl.BlockSpec((1, CB), lambda i: (0, i + offset)),
        ],
        out_specs=pl.BlockSpec((ROWS, CB), lambda i: (0, i)),
        scratch_shapes=[
            pltpu.VMEM((EXT, vocab), jnp.bfloat16),
            pltpu.VMEM((EXT, LANES), jnp.float32),
            pltpu.VMEM((EXT, LANES), jnp.float32),
            pltpu.VMEM((3, EXT + 8, CB), jnp.float32),
            pltpu.VMEM((EXT, CB), jnp.float32),
            pltpu.VMEM((TAPS + R, LANES), jnp.float32),
            pltpu.VMEM((TAPS, CB), jnp.float32),
            pltpu.VMEM((ROWS, CB), jnp.float32),
            pltpu.SMEM((MAX_PAIRS,), jnp.int32),
            pltpu.SMEM((MAX_PAIRS,), jnp.int32),
            pltpu.SMEM((MAX_PAIRS,), jnp.int32),
            pltpu.SMEM((1,), jnp.int32),
        ],
        compiler_params=pltpu.CompilerParams(vmem_limit_bytes=40 * 2**20),
        cost_estimate=pl.CostEstimate(
            flops=2 * EXT * vocab * 3 * count + 100 * 2 * ROWS * count * TAPS,
            bytes_accessed=6 * vocab * count + 2 * ROWS * count,
            transcendentals=0,
        ),
    )(begin, end, ids, age, table, short_filter, mr_filter, mr_decay)


def body(
    token_ids,
    subst_pos,
    subst_base,
    window_lengths,
    embed_table,
    norm_gain,
    in_weight,
    short_filter,
    mr_filter,
    mr_decay,
    out_weight,
):
    row_count = token_ids.shape[0]
    channels = in_weight.shape[2]
    depth = in_weight.shape[0]
    vocab, width = embed_table.shape
    parts = lax.axis_size("context")
    copies = lax.axis_size("dp")
    each = channels // (parts * copies)

    shares = in_weight.reshape(depth, 3, parts, copies, each)
    shares = lax.dynamic_index_in_dim(shares, lax.axis_index("dp"), 3, keepdims=False)
    shares = shares.transpose(2, 1, 3, 0).reshape(parts, 3 * each, depth)
    shares = lax.all_to_all(shares, "context", 0, 0, tiled=True)
    x_wide = embed_table.astype(jnp.float32)
    scale = lax.rsqrt(jnp.mean(x_wide * x_wide, axis=1, keepdims=True) + 1e-06)
    normed = (x_wide * scale * norm_gain[None, :]).astype(jnp.bfloat16)
    own_weight = shares.transpose(1, 0, 2).reshape(3 * each, width)
    table = lax.dot_general(own_weight, normed, (((1,), (1,)), ((), ())), preferred_element_type=jnp.float32)
    table = lax.all_gather(table.astype(jnp.bfloat16), ("context", "dp"), axis=0, tiled=True)
    table = table.reshape(parts * copies, 3, each, vocab)

    matches = subst_pos[:, None] == jnp.arange(row_count, dtype=jnp.int32)[None, :]
    chosen = jnp.sum(jnp.where(matches, subst_base[:, None], 0), axis=0)
    touched = jnp.any(matches, axis=0)
    new_ids = jnp.where(touched, chosen, token_ids)
    before = passed_along(new_ids[row_count - HALO :], "context", 1)
    ids = jnp.concatenate([before, new_ids])

    first_row = lax.axis_index("context") * row_count - HALO
    ends = jnp.cumsum(window_lengths)
    starts = ends - window_lengths
    positions = first_row + jnp.arange(EXT, dtype=jnp.int32)
    begins = jnp.max(jnp.where(starts[None, :] <= positions[:, None], starts[None, :], -1), axis=1)
    age = jnp.where(begins >= 0, positions - begins, -1)

    def part(first, count):
        return gated_rows(
            starts - first_row,
            ends - first_row,
            ids[:, None],
            age[:, None],
            table,
            short_filter,
            mr_filter,
            mr_decay[None, :],
            first,
            count,
        )

    weight_in, table = lax.optimization_barrier((out_weight, table))
    weight_rows = lax.all_gather(weight_in, "context", axis=0, tiled=True)
    tensors = lax.axis_size("tensor")
    weight_rows = weight_rows.reshape(tensors, channels, out_weight.shape[1])
    own_columns = lax.dynamic_slice_in_dim(
        embed_table, lax.axis_index("tensor") * out_weight.shape[1], out_weight.shape[1], 1
    )
    picked = (new_ids[:, None] == jnp.arange(vocab, dtype=jnp.int32)[None, :]).astype(jnp.bfloat16)
    total = jnp.dot(picked, own_columns, preferred_element_type=jnp.float32)
    for first in range(0, channels, CB):
        features = lax.all_gather(part(first, CB), "tensor", axis=1, tiled=True)
        rows = weight_rows[:, first : first + CB].reshape(tensors * CB, -1)
        total = total + jnp.dot(features, rows, preferred_element_type=jnp.float32)
    return total.astype(jnp.bfloat16)


def solution(mesh):
    in_specs = (
        P(("dp", "context")),
        P(("dp", "context")),
        P(("dp", "context")),
        P("dp"),
        P(),
        P(),
        P("context", None, "tensor"),
        P(None, None, "tensor"),
        P(None, "tensor"),
        P("tensor"),
        P("context", "tensor"),
    )
    out_specs = P(("dp", "context"), "tensor")
    return jax.shard_map(body, mesh=mesh, in_specs=in_specs, out_specs=out_specs, check_vma=False)
```

```python
import jax
import jax.numpy as jnp
from jax import lax
from jax.experimental import pallas as pl
from jax.experimental.pallas import tpu as pltpu
from jax.sharding import PartitionSpec as P

ROWS = 768
HALO = 144
EXT = HALO + ROWS
TAPS = 128
LANES = 128
R = 32
PIECES = ROWS // R
GROUP = 4
DEPTH = 256
SIDE = 4
PEERS = SIDE * SIDE
CHUNKS = 8
SHARE = 3 * LANES * CHUNKS // (2 * PEERS)
HALF = ROWS // 2
MESH = pl.DeviceIdType.MESH


def moved(c, k, sign):
    x = lax.rem(c // SIDE + SIDE + sign * (k // SIDE), SIDE)
    z = lax.rem(lax.rem(c, SIDE) + SIDE + sign * (k % SIDE), SIDE)
    return x * SIDE + z


def greet(axis_targets):
    barrier = pltpu.get_barrier_semaphore()
    for target in axis_targets:
        pl.semaphore_signal(barrier, inc=1, device_id=target, device_id_type=MESH)
    pl.semaphore_wait(barrier, len(axis_targets))


def send(source, target, sent, arrived, where):
    return pltpu.make_async_remote_copy(
        src_ref=source, dst_ref=target, send_sem=sent, recv_sem=arrived, device_id=where, device_id_type=MESH
    )


def table_kernel(
    shares,
    embed,
    gain,
    ids,
    table,
    before,
    got,
    normed,
    piece,
    sent_w,
    come_w,
    sent_t,
    come_t,
    sent_f,
    come_f,
    ids_sem,
    local_sem,
):
    d = lax.axis_index("dp")
    c = lax.axis_index("context")
    other = {"dp": 1 - d}
    following = lax.rem(c + 1, PEERS)
    previous = lax.rem(c + PEERS - 1, PEERS)
    greet(
        [{"context": moved(c, k, 1)} for k in range(1, PEERS)]
        + [other, {"context": following}, {"context": previous}]
    )
    weights = [
        send(shares.at[moved(c, k, 1)], got.at[c], sent_w.at[k], come_w.at[k], {"context": moved(c, k, 1)})
        for k in range(1, PEERS)
    ]
    for copy in weights:
        copy.start()
    ids_copy = send(ids, before, ids_sem.at[0], ids_sem.at[1], {"context": following})
    ids_copy.start()

    vocab, width = embed.shape
    step = 32

    def norm_rows(i, carry):
        rows = pl.ds(pl.multiple_of(i * step, step), step)
        wide = embed[rows, :].astype(jnp.float32)
        scale = lax.rsqrt(jnp.mean(wide * wide, axis=1, keepdims=True) + 1e-06)
        values = (wide * scale * gain[...]).astype(jnp.bfloat16)
        for s in range(PEERS):
            normed[s, rows, :] = values[:, s * DEPTH : (s + 1) * DEPTH]
        return carry

    lax.fori_loop(0, vocab // step, norm_rows, 0)

    def product(weight, s):
        return lax.dot_general(
            weight, normed[s], (((1,), (1,)), ((), ())), preferred_element_type=jnp.float32
        )

    total = product(shares[c], c)
    for k in range(1, PEERS):
        weights[k - 1].wait_recv()
        origin = moved(c, k, -1)
        total = total + product(got[origin], origin)
    piece[...] = total.astype(jnp.bfloat16)
    mine = table.at[2 * c + d]
    spread = [
        send(piece, mine, sent_t.at[k], come_t.at[k], {"context": moved(c, k, 1)}) for k in range(1, PEERS)
    ]
    forward = [send(piece, mine, sent_f.at[0], come_f.at[0], other)]
    forward[0].start()
    for copy in spread:
        copy.start()
    local = pltpu.make_async_copy(piece, mine, local_sem)
    local.start()
    for k in range(1, PEERS):
        spread[k - 1].wait_recv()
        slot = table.at[2 * moved(c, k, -1) + d]
        forward.append(send(slot, slot, sent_f.at[k], come_f.at[k], other))
        forward[k].start()
    for copy in forward:
        copy.wait_recv()
    for copy in weights + spread + forward:
        copy.wait_send()
    ids_copy.wait()
    local.wait()


def token_table(shares, embed, gain, ids):
    vmem = pl.BlockSpec(memory_space=pltpu.VMEM)
    anywhere = pl.BlockSpec(memory_space=pl.ANY)
    vocab, width = embed.shape
    semaphores = [pltpu.SemaphoreType.DMA((PEERS,))] * 6
    return pl.pallas_call(
        table_kernel,
        out_shape=(
            jax.ShapeDtypeStruct((2 * PEERS, SHARE, vocab), jnp.bfloat16),
            jax.ShapeDtypeStruct(ids.shape, jnp.int32),
        ),
        in_specs=[vmem, vmem, vmem, anywhere],
        out_specs=(anywhere, anywhere),
        scratch_shapes=[
            pltpu.VMEM((PEERS, SHARE, DEPTH), jnp.bfloat16),
            pltpu.VMEM((PEERS, vocab, DEPTH), jnp.bfloat16),
            pltpu.VMEM((SHARE, vocab), jnp.bfloat16),
            *semaphores,
            pltpu.SemaphoreType.DMA((2,)),
            pltpu.SemaphoreType.DMA,
        ],
        compiler_params=pltpu.CompilerParams(
            collective_id=0, has_side_effects=True, vmem_limit_bytes=40 * 2**20
        ),
        cost_estimate=pl.CostEstimate(flops=2 * SHARE * vocab * width, bytes_accessed=2**24, transcendentals=0),
    )(shares, embed, gain, ids)


def block_kernel(
    begin_ref,
    end_ref,
    ids_ref,
    age_ref,
    table,
    short_ref,
    filt_ref,
    decay_ref,
    columns,
    weight,
    out_ref,
    onehot,
    mask1,
    mask2,
    src,
    prod,
    window,
    taps,
    longs,
    gates,
    total,
    weights,
    sent_own,
    come_own,
    sent_pass,
    come_pass,
    sent_w,
    come_w,
    sent_f,
    come_f,
    local_sem,
):
    d = lax.axis_index("dp")
    c = lax.axis_index("context")
    t = lax.axis_index("tensor")
    right = lax.rem(t + 1, SIDE)
    left = lax.rem(t + SIDE - 1, SIDE)
    other = {"dp": 1 - d}
    greet(
        [{"tensor": right}, {"tensor": left}, other]
        + [{"context": moved(c, k, 1)} for k in range(1, PEERS)]
    )
    spread = [
        send(weight.at[d], weights.at[2 * c + d], sent_w.at[k], come_w.at[k], {"context": moved(c, k, 1)})
        for k in range(1, PEERS)
    ]
    for copy in spread:
        copy.start()
    local = [pltpu.make_async_copy(weight.at[h], weights.at[2 * c + h], local_sem.at[h]) for h in range(2)]
    for copy in local:
        copy.start()

    vocab = onehot.shape[1]
    ids = jnp.broadcast_to(ids_ref[...], (EXT, vocab))
    onehot[...] = jnp.where(ids == lax.broadcasted_iota(jnp.int32, (EXT, vocab), 1), 1.0, 0.0).astype(jnp.bfloat16)
    age = jnp.broadcast_to(age_ref[...], (EXT, LANES))
    mask1[...] = (age >= 1).astype(jnp.float32)
    mask2[...] = (age >= 2).astype(jnp.float32)
    src[0:8, :] = jnp.zeros((8, 3 * LANES), jnp.float32)

    def own_copies(i):
        return (
            send(gates.at[t, i], gates.at[t, i], sent_own.at[0, i], come_own.at[0, i], {"tensor": right}),
            send(gates.at[t, i], gates.at[t, i], sent_own.at[1, i], come_own.at[1, i], {"tensor": left}),
        )

    def pass_copies(i):
        low = (i, pl.ds(0, HALF))
        high = (i, pl.ds(HALF, HALF))
        return (
            send(gates.at[left, *low], gates.at[left, *low], sent_pass.at[0, i], come_pass.at[0, i], {"tensor": right}),
            send(gates.at[right, *high], gates.at[right, *high], sent_pass.at[1, i], come_pass.at[1, i], {"tensor": left}),
        )

    def hand_on(i):
        own, further = own_copies(i), pass_copies(i)
        for direction in range(2):
            own[direction].wait_recv()
            further[direction].start()

    def chunk(i, carry):
        pieces = table[pl.ds(i * 4, 4)].reshape(3 * LANES, vocab)
        src[8:, :] = lax.dot_general(
            onehot[...], pieces, (((1,), (1,)), ((), ())), preferred_element_type=jnp.float32
        )
        tap_index = lax.broadcasted_iota(jnp.int32, (TAPS, LANES), 0).astype(jnp.float32)
        taps[...] = filt_ref[i] * jnp.exp(-decay_ref[i] * tap_index)
        filters = short_ref[i]

        def mixed(g, low, count):
            lanes = slice(g * LANES, (g + 1) * LANES)
            return (
                filters[0, g : g + 1] * src[pl.ds(8 + low, count), lanes]
                + filters[1, g : g + 1] * (src[pl.ds(7 + low, count), lanes] * mask1[pl.ds(low, count), :])
                + filters[2, g : g + 1] * (src[pl.ds(6 + low, count), lanes] * mask2[pl.ds(low, count), :])
            )

        for low in range(0, EXT, 48):
            product = mixed(1, low, 48) * mixed(2, low, 48)
            prod[pl.ds(low, 48), :] = product.astype(jnp.bfloat16).astype(jnp.float32)

        def piece(n, carry):
            row = pl.multiple_of(HALO + n * R, 16)
            begin = begin_ref[n]
            end = end_ref[n]
            at = row - TAPS + lax.broadcasted_iota(jnp.int32, (TAPS + R, LANES), 0)
            inside = (at >= begin) & (at < end)
            values = prod[pl.ds(row - TAPS, TAPS + R), :]
            window[0] = jnp.where(inside, values, 0.0)
            window[1, TAPS - 8 :] = values[TAPS - 8 :]
            ages = jnp.broadcast_to(age_ref[pl.ds(row, R), :], (R, LANES))
            sums = [jnp.zeros((8, LANES), jnp.float32) for _ in range(R // 8)]
            late = [jnp.zeros((8, LANES), jnp.float32) for _ in range(R // 8)]
            for phase in range(8):
                for block in range(0, TAPS // 8, GROUP):
                    held = [
                        jnp.broadcast_to(taps[pl.ds(phase + 8 * (block + m), 1), :], (8, LANES))
                        for m in range(GROUP)
                    ]
                    views = {
                        q: window[0, pl.ds(TAPS + 8 * q - phase, 8), :]
                        for q in range(-(block + GROUP - 1), R // 8 - block)
                    }
                    for i in range(R // 8):
                        for m in range(GROUP):
                            sums[i] = sums[i] + held[m] * views[i - block - m]
                    if block < R // 8:
                        starts = {q: window[1, pl.ds(TAPS + 8 * q - phase, 8), :] for q in range(R // 8)}
                        for i in range(R // 8):
                            for m in range(GROUP):
                                q = i - block - m
                                if q < 0:
                                    continue
                                kept = ages[8 * i : 8 * i + 8] >= phase + 8 * (block + m)
                                late[i] = late[i] + held[m] * jnp.where(kept, starts[q], 0.0)
            result = jnp.where(
                at[TAPS:] < end, jnp.concatenate(sums, axis=0), jnp.concatenate(late, axis=0)
            )
            longs[pl.ds(pl.multiple_of(n * R, R), R), :] = result
            return carry

        lax.fori_loop(0, PIECES, piece, 0)
        for low in range(0, ROWS, 48):
            gated = mixed(0, HALO + low, 48) * longs[pl.ds(low, 48), :]
            gates[t, i, pl.ds(low, 48), :] = gated.astype(jnp.bfloat16)
        for copy in own_copies(i):
            copy.start()

        @pl.when(i > 0)
        def _():
            hand_on(i - 1)

        return carry

    lax.fori_loop(0, CHUNKS, chunk, 0)
    hand_on(CHUNKS - 1)

    forward = []
    for k in range(1, PEERS):
        spread[k - 1].wait_recv()
        slot = weights.at[2 * moved(c, k, -1) + d]
        forward.append(send(slot, slot, sent_f.at[k], come_f.at[k], other))
        forward[k - 1].start()
    total[...] = jnp.dot(onehot[HALO:, :], columns[...], preferred_element_type=jnp.float32)
    for copy in local:
        copy.wait()
    for copy in forward:
        copy.wait_recv()

    def finish(i, carry):
        for copy in pass_copies(i):
            copy.wait_recv()
        features = jnp.concatenate([gates[s, i] for s in range(SIDE)], axis=1)
        rows = jnp.concatenate([weights[s * CHUNKS + i] for s in range(SIDE)], axis=0)
        total[...] += jnp.dot(features, rows, preferred_element_type=jnp.float32)
        return carry

    lax.fori_loop(0, CHUNKS, finish, 0)
    out_ref[...] = total[...].astype(jnp.bfloat16)

    def drain(i, carry):
        for copy in own_copies(i) + pass_copies(i):
            copy.wait_send()
        return carry

    lax.fori_loop(0, CHUNKS, drain, 0)
    for copy in spread + forward:
        copy.wait_send()


def block_rows(begin, end, ids, age, table, short_filter, mr_filter, mr_decay, columns, weight):
    vocab = table.shape[2]
    width = columns.shape[1]
    smem = pl.BlockSpec(memory_space=pltpu.SMEM)
    vmem = pl.BlockSpec(memory_space=pltpu.VMEM)
    return pl.pallas_call(
        block_kernel,
        out_shape=jax.ShapeDtypeStruct((ROWS, width), jnp.bfloat16),
        in_specs=[smem, smem] + [vmem] * 8,
        out_specs=vmem,
        scratch_shapes=[
            pltpu.VMEM((EXT, vocab), jnp.bfloat16),
            pltpu.VMEM((EXT, LANES), jnp.float32),
            pltpu.VMEM((EXT, LANES), jnp.float32),
            pltpu.VMEM((EXT + 8, 3 * LANES), jnp.float32),
            pltpu.VMEM((EXT, LANES), jnp.float32),
            pltpu.VMEM((2, TAPS + R, LANES), jnp.float32),
            pltpu.VMEM((TAPS, LANES), jnp.float32),
            pltpu.VMEM((ROWS, LANES), jnp.float32),
            pltpu.VMEM((SIDE, CHUNKS, ROWS, LANES), jnp.bfloat16),
            pltpu.VMEM((ROWS, width), jnp.float32),
            pltpu.VMEM((2 * PEERS, DEPTH // 2, width), jnp.bfloat16),
            pltpu.SemaphoreType.DMA((2, CHUNKS)),
            pltpu.SemaphoreType.DMA((2, CHUNKS)),
            pltpu.SemaphoreType.DMA((2, CHUNKS)),
            pltpu.SemaphoreType.DMA((2, CHUNKS)),
            pltpu.SemaphoreType.DMA((PEERS,)),
            pltpu.SemaphoreType.DMA((PEERS,)),
            pltpu.SemaphoreType.DMA((PEERS,)),
            pltpu.SemaphoreType.DMA((PEERS,)),
            pltpu.SemaphoreType.DMA((2,)),
        ],
        compiler_params=pltpu.CompilerParams(
            collective_id=1, has_side_effects=True, vmem_limit_bytes=56 * 2**20
        ),
        cost_estimate=pl.CostEstimate(flops=2 * ROWS * width * 4096, bytes_accessed=2**24, transcendentals=0),
    )(begin, end, ids, age, table, short_filter, mr_filter, mr_decay, columns, weight)


def body(
    token_ids,
    subst_pos,
    subst_base,
    window_lengths,
    embed_table,
    norm_gain,
    in_weight,
    short_filter,
    mr_filter,
    mr_decay,
    out_weight,
):
    row_count = token_ids.shape[0]
    vocab = embed_table.shape[0]
    width = out_weight.shape[1]

    matches = subst_pos[:, None] == jnp.arange(row_count, dtype=jnp.int32)[None, :]
    chosen = jnp.sum(jnp.where(matches, subst_base[:, None], 0), axis=0)
    touched = jnp.any(matches, axis=0)
    new_ids = jnp.where(touched, chosen, token_ids)

    shares = in_weight.reshape(DEPTH, 3, CHUNKS, LANES).transpose(2, 1, 3, 0).reshape(PEERS, 2, SHARE, DEPTH)
    shares = lax.dynamic_index_in_dim(shares, lax.axis_index("dp"), 1, keepdims=False)
    table, before = token_table(shares, embed_table, norm_gain[None, :], new_ids.reshape(-1, LANES))
    ids = jnp.concatenate([before.reshape(-1)[row_count - HALO :], new_ids])

    first_row = lax.axis_index("context") * row_count - HALO
    ends = jnp.cumsum(window_lengths)
    starts = ends - window_lengths
    positions = first_row + jnp.arange(EXT, dtype=jnp.int32)
    begins = jnp.max(jnp.where(starts[None, :] <= positions[:, None], starts[None, :], -1), axis=1)
    age = jnp.where(begins >= 0, positions - begins, -1)
    heads = first_row + HALO + R * jnp.arange(PIECES, dtype=jnp.int32)
    head_begin = jnp.max(jnp.where(starts[None, :] <= heads[:, None], starts[None, :], -1), axis=1)
    head_end = jnp.min(jnp.where(ends[None, :] > heads[:, None], ends[None, :], 1 << 20), axis=1)

    columns = lax.dynamic_slice_in_dim(embed_table, lax.axis_index("tensor") * width, width, 1)
    return block_rows(
        head_begin - first_row,
        head_end - first_row,
        ids[:, None],
        age[:, None],
        table,
        short_filter.reshape(3, 3, CHUNKS, LANES).transpose(2, 0, 1, 3),
        mr_filter.reshape(TAPS, CHUNKS, LANES).transpose(1, 0, 2),
        mr_decay.reshape(CHUNKS, 1, LANES),
        columns,
        out_weight.reshape(2, DEPTH // 2, width),
    )


def solution(mesh):
    in_specs = (
        P(("dp", "context")),
        P(("dp", "context")),
        P(("dp", "context")),
        P("dp"),
        P(),
        P(),
        P("context", None, "tensor"),
        P(None, None, "tensor"),
        P(None, "tensor"),
        P("tensor"),
        P("context", "tensor"),
    )
    out_specs = P(("dp", "context"), "tensor")
    return jax.shard_map(body, mesh=mesh, in_specs=in_specs, out_specs=out_specs, check_vma=False)
```

```python
import jax
import jax.numpy as jnp
from jax import lax
from jax.experimental import pallas as pl
from jax.experimental.pallas import tpu as pltpu
from jax.sharding import PartitionSpec as P

ROWS = 768
HALO = 144
EXT = HALO + ROWS
TAPS = 128
LANES = 128
R = 32
PIECES = ROWS // R
GROUP = 4
DEPTH = 256
SIDE = 4
PEERS = SIDE * SIDE
CHUNKS = 8
SHARE = 3 * LANES * CHUNKS // (2 * PEERS)
HALF = ROWS // 2
MESH = pl.DeviceIdType.MESH


def moved(c, k, sign):
    x = lax.rem(c // SIDE + SIDE + sign * (k // SIDE), SIDE)
    z = lax.rem(lax.rem(c, SIDE) + SIDE + sign * (k % SIDE), SIDE)
    return x * SIDE + z


def greet(axis_targets):
    barrier = pltpu.get_barrier_semaphore()
    for target in axis_targets:
        pl.semaphore_signal(barrier, inc=1, device_id=target, device_id_type=MESH)
    pl.semaphore_wait(barrier, len(axis_targets))


def send(source, target, sent, arrived, where):
    return pltpu.make_async_remote_copy(
        src_ref=source, dst_ref=target, send_sem=sent, recv_sem=arrived, device_id=where, device_id_type=MESH
    )


class Ring:
    def __init__(self, buffer, half, sent, come):
        d = lax.axis_index("dp")
        c = lax.axis_index("context")
        self.x, self.z, self.d = c // SIDE, lax.rem(c, SIDE), d
        self.buffer, self.sent, self.come = buffer, sent, come
        self.low, self.high = pl.ds(0, half), pl.ds(half, half)

    def context(self, j, m):
        dx = (1 - self.d) * m + self.d * j
        dz = (1 - self.d) * j + self.d * m
        return lax.rem(self.x + dx, SIDE) * SIDE + lax.rem(self.z + dz, SIDE)

    def copy(self, j, m, part, index, where):
        at = 2 * self.context(j, m) + self.d
        slot = self.buffer.at[at] if part is None else self.buffer.at[at, part]
        return send(slot, slot, self.sent.at[index], self.come.at[index], where)

    def along_a(self, side):
        return {"context": self.context(3 if side else 1, 0)}

    def along_b(self, side):
        return {"context": self.context(0, 3 if side else 1)}

    def first(self, side):
        return self.copy(0, 0, None, side, self.along_a(side))

    def second(self, side):
        return self.copy(1 if side else 3, 0, self.high if side else self.low, 2 + side, self.along_a(side))

    def third(self, j, side):
        return self.copy(j, 0, None, 4 + 2 * j + side, self.along_b(side))

    def fourth(self, j, side):
        return self.copy(
            j, 1 if side else 3, self.high if side else self.low, 12 + 2 * j + side, self.along_b(side)
        )

    def across(self, j, m):
        return self.copy(j, m, None, 20 + 4 * j + m, {"dp": 1 - self.d})

    def cross(self, *slots):
        for j, m in slots:
            self.across(j, m).start()

    def crossed(self, *slots):
        for j, m in slots:
            self.across(j, m).wait_recv()

    def hop1(self):
        for side in range(2):
            self.first(side).start()
            self.third(0, side).start()

    def hop2(self):
        for side in range(2):
            self.first(side).wait_recv()
            self.second(side).start()
            self.third(0, side).wait_recv()
            self.fourth(0, side).start()
        self.cross(*self.set2)
        for j in (1, 3):
            for side in range(2):
                self.third(j, side).start()

    def hop3(self):
        for side in range(2):
            self.second(side).wait_recv()
        for side in range(2):
            self.third(2, side).start()
        for side in range(2):
            self.fourth(0, side).wait_recv()
        for j in (1, 3):
            for side in range(2):
                self.third(j, side).wait_recv()
                self.fourth(j, side).start()
        self.cross(*self.set3)

    def hop4(self):
        for side in range(2):
            self.third(2, side).wait_recv()
            self.fourth(2, side).start()
        for j in (1, 3):
            for side in range(2):
                self.fourth(j, side).wait_recv()
        self.cross(*self.set4)

    def hop5(self):
        for side in range(2):
            self.fourth(2, side).wait_recv()
        self.cross(*self.set5)

    set2 = ((1, 0), (3, 0), (0, 1), (0, 3))
    set3 = ((2, 0), (0, 2), (1, 1), (1, 3), (3, 1), (3, 3))
    set4 = ((2, 1), (2, 3), (1, 2), (3, 2))
    set5 = ((2, 2),)

    def drain(self):
        for side in range(2):
            self.first(side).wait_send()
            self.second(side).wait_send()
            for j in range(SIDE):
                self.third(j, side).wait_send()
                self.fourth(j, side).wait_send()
        for j, m in self.set2 + self.set3 + self.set4 + self.set5:
            self.across(j, m).wait_send()


def table_kernel(
    shares,
    embed,
    gain,
    ids,
    table,
    before,
    got,
    normed,
    piece,
    sent_w,
    come_w,
    sent_t,
    come_t,
    sent_f,
    come_f,
    ids_sem,
    local_sem,
):
    d = lax.axis_index("dp")
    c = lax.axis_index("context")
    other = {"dp": 1 - d}
    following = lax.rem(c + 1, PEERS)
    previous = lax.rem(c + PEERS - 1, PEERS)
    greet(
        [{"context": moved(c, k, 1)} for k in range(1, PEERS)]
        + [other, {"context": following}, {"context": previous}]
    )
    weights = [
        send(shares.at[moved(c, k, 1)], got.at[c], sent_w.at[k], come_w.at[k], {"context": moved(c, k, 1)})
        for k in range(1, PEERS)
    ]
    for copy in weights:
        copy.start()
    ids_copy = send(ids, before, ids_sem.at[0], ids_sem.at[1], {"context": following})
    ids_copy.start()

    vocab, width = embed.shape
    step = 32

    def norm_rows(i, carry):
        rows = pl.ds(pl.multiple_of(i * step, step), step)
        wide = embed[rows, :].astype(jnp.float32)
        scale = lax.rsqrt(jnp.mean(wide * wide, axis=1, keepdims=True) + 1e-06)
        values = (wide * scale * gain[...]).astype(jnp.bfloat16)
        for s in range(PEERS):
            normed[s, rows, :] = values[:, s * DEPTH : (s + 1) * DEPTH]
        return carry

    lax.fori_loop(0, vocab // step, norm_rows, 0)

    def product(weight, s):
        return lax.dot_general(
            weight, normed[s], (((1,), (1,)), ((), ())), preferred_element_type=jnp.float32
        )

    total = product(shares[c], c)
    for k in range(1, PEERS):
        weights[k - 1].wait_recv()
        origin = moved(c, k, -1)
        total = total + product(got[origin], origin)
    piece[...] = total.astype(jnp.bfloat16)
    mine = table.at[2 * c + d]
    spread = [
        send(piece, mine, sent_t.at[k], come_t.at[k], {"context": moved(c, k, 1)}) for k in range(1, PEERS)
    ]
    forward = [send(piece, mine, sent_f.at[0], come_f.at[0], other)]
    forward[0].start()
    for copy in spread:
        copy.start()
    local = pltpu.make_async_copy(piece, mine, local_sem)
    local.start()
    for k in range(1, PEERS):
        spread[k - 1].wait_recv()
        slot = table.at[2 * moved(c, k, -1) + d]
        forward.append(send(slot, slot, sent_f.at[k], come_f.at[k], other))
        forward[k].start()
    for copy in forward:
        copy.wait_recv()
    for copy in weights + spread + forward:
        copy.wait_send()
    ids_copy.wait()
    local.wait()


def token_table(shares, embed, gain, ids):
    vmem = pl.BlockSpec(memory_space=pltpu.VMEM)
    anywhere = pl.BlockSpec(memory_space=pl.ANY)
    vocab, width = embed.shape
    semaphores = [pltpu.SemaphoreType.DMA((PEERS,))] * 6
    return pl.pallas_call(
        table_kernel,
        out_shape=(
            jax.ShapeDtypeStruct((2 * PEERS, SHARE, vocab), jnp.bfloat16),
            jax.ShapeDtypeStruct(ids.shape, jnp.int32),
        ),
        in_specs=[vmem, vmem, vmem, anywhere],
        out_specs=(anywhere, anywhere),
        scratch_shapes=[
            pltpu.VMEM((PEERS, SHARE, DEPTH), jnp.bfloat16),
            pltpu.VMEM((PEERS, vocab, DEPTH), jnp.bfloat16),
            pltpu.VMEM((SHARE, vocab), jnp.bfloat16),
            *semaphores,
            pltpu.SemaphoreType.DMA((2,)),
            pltpu.SemaphoreType.DMA,
        ],
        compiler_params=pltpu.CompilerParams(
            collective_id=0, has_side_effects=True, vmem_limit_bytes=40 * 2**20
        ),
        cost_estimate=pl.CostEstimate(flops=2 * SHARE * vocab * width, bytes_accessed=2**24, transcendentals=0),
    )(shares, embed, gain, ids)


def block_kernel(
    begin_ref,
    end_ref,
    ids_ref,
    age_ref,
    table,
    short_ref,
    filt_ref,
    decay_ref,
    columns,
    weight,
    out_ref,
    onehot,
    mask1,
    mask2,
    src,
    prod,
    window,
    recent,
    taps,
    longs,
    gates,
    total,
    weights,
    sent_own,
    come_own,
    sent_pass,
    come_pass,
    sent_w,
    come_w,
    local_sem,
):
    d = lax.axis_index("dp")
    c = lax.axis_index("context")
    t = lax.axis_index("tensor")
    right = lax.rem(t + 1, SIDE)
    left = lax.rem(t + SIDE - 1, SIDE)
    other = {"dp": 1 - d}
    greet(
        [{"tensor": right}, {"tensor": left}, other]
        + [{"context": moved(c, k, 1)} for k in range(1, PEERS)]
    )
    local = [pltpu.make_async_copy(weight.at[h], weights.at[2 * c + h], local_sem.at[h]) for h in range(2)]
    for copy in local:
        copy.start()
    outs = Ring(weights, LANES // 2, sent_w, come_w)

    vocab = onehot.shape[1]
    ids = jnp.broadcast_to(ids_ref[...], (EXT, vocab))
    onehot[...] = jnp.where(ids == lax.broadcasted_iota(jnp.int32, (EXT, vocab), 1), 1.0, 0.0).astype(jnp.bfloat16)
    age = jnp.broadcast_to(age_ref[...], (EXT, LANES))
    mask1[...] = (age >= 1).astype(jnp.float32)
    mask2[...] = (age >= 2).astype(jnp.float32)
    src[0:8, :] = jnp.zeros((8, 3 * LANES), jnp.float32)
    for copy in local:
        copy.wait()
    outs.hop1()

    def own_copies(i):
        return (
            send(gates.at[t, i], gates.at[t, i], sent_own.at[0, i], come_own.at[0, i], {"tensor": right}),
            send(gates.at[t, i], gates.at[t, i], sent_own.at[1, i], come_own.at[1, i], {"tensor": left}),
        )

    def pass_copies(i):
        low = (i, pl.ds(0, HALF))
        high = (i, pl.ds(HALF, HALF))
        return (
            send(gates.at[left, *low], gates.at[left, *low], sent_pass.at[0, i], come_pass.at[0, i], {"tensor": right}),
            send(gates.at[right, *high], gates.at[right, *high], sent_pass.at[1, i], come_pass.at[1, i], {"tensor": left}),
        )

    def hand_on(i):
        own, further = own_copies(i), pass_copies(i)
        for direction in range(2):
            own[direction].wait_recv()
            further[direction].start()

    def chunk(i, carry):
        for at, hop in ((1, outs.hop2), (2, outs.hop3), (4, outs.hop4), (5, outs.hop5)):
            pl.when(i == at)(hop)

        pieces = table[pl.ds(i * 4, 4)].reshape(3 * LANES, vocab)
        src[8:, :] = lax.dot_general(
            onehot[...], pieces, (((1,), (1,)), ((), ())), preferred_element_type=jnp.float32
        )
        tap_index = lax.broadcasted_iota(jnp.int32, (TAPS, LANES), 0).astype(jnp.float32)
        taps[...] = filt_ref[i] * jnp.exp(-decay_ref[i] * tap_index)
        filters = short_ref[i]

        def mixed(g, low, count):
            lanes = slice(g * LANES, (g + 1) * LANES)
            return (
                filters[0, g : g + 1] * src[pl.ds(8 + low, count), lanes]
                + filters[1, g : g + 1] * (src[pl.ds(7 + low, count), lanes] * mask1[pl.ds(low, count), :])
                + filters[2, g : g + 1] * (src[pl.ds(6 + low, count), lanes] * mask2[pl.ds(low, count), :])
            )

        for low in range(0, EXT, 48):
            product = mixed(1, low, 48) * mixed(2, low, 48)
            prod[pl.ds(low, 48), :] = product.astype(jnp.bfloat16).astype(jnp.float32)

        def piece(n, carry):
            row = pl.multiple_of(HALO + n * R, 16)
            begin = begin_ref[n]
            end = end_ref[n]
            before = row - TAPS + lax.broadcasted_iota(jnp.int32, (TAPS, LANES), 0)
            window[...] = jnp.where(before >= begin, prod[pl.ds(row - TAPS, TAPS), :], 0.0)
            recent[...] = prod[pl.ds(row - 8, R + 8), :]
            age = jnp.broadcast_to(age_ref[pl.ds(row, R), :], (R, LANES))
            sums = [jnp.zeros((8, LANES), jnp.float32) for _ in range(R // 8)]
            near = [jnp.zeros((8, LANES), jnp.float32) for _ in range(R // 8)]
            for phase in range(8):
                for block in range(0, TAPS // 8, GROUP):
                    held = [
                        jnp.broadcast_to(taps[pl.ds(phase + 8 * (block + m), 1), :], (8, LANES))
                        for m in range(GROUP)
                    ]
                    views = {
                        q: window[pl.ds(TAPS + 8 * q - phase, 8), :]
                        if q < 0
                        else recent[pl.ds(8 + 8 * q - phase, 8), :]
                        for q in range(-(block + GROUP - 1), R // 8 - block)
                    }
                    for i in range(R // 8):
                        for m in range(GROUP):
                            q = i - block - m
                            if q < 0:
                                sums[i] = sums[i] + held[m] * views[q]
                            else:
                                kept = age[8 * i : 8 * i + 8] >= phase + 8 * (block + m)
                                near[i] = near[i] + held[m] * jnp.where(kept, views[q], 0.0)
            mine = row + lax.broadcasted_iota(jnp.int32, (R, LANES), 0) < end
            result = jnp.where(mine, jnp.concatenate(sums, axis=0), 0.0) + jnp.concatenate(near, axis=0)
            longs[pl.ds(pl.multiple_of(n * R, R), R), :] = result
            return carry

        lax.fori_loop(0, PIECES, piece, 0)
        for low in range(0, ROWS, 48):
            gated = mixed(0, HALO + low, 48) * longs[pl.ds(low, 48), :]
            gates[t, i, pl.ds(low, 48), :] = gated.astype(jnp.bfloat16)
        for copy in own_copies(i):
            copy.start()

        @pl.when(i > 0)
        def _():
            hand_on(i - 1)

        return carry

    lax.fori_loop(0, CHUNKS, chunk, 0)
    hand_on(CHUNKS - 1)

    total[...] = jnp.dot(onehot[HALO:, :], columns[...], preferred_element_type=jnp.float32)
    outs.crossed(*Ring.set2, *Ring.set3, *Ring.set4, *Ring.set5)

    def finish(i, carry):
        for copy in pass_copies(i):
            copy.wait_recv()
        features = jnp.concatenate([gates[s, i] for s in range(SIDE)], axis=1)
        rows = jnp.concatenate([weights[s * CHUNKS + i] for s in range(SIDE)], axis=0)
        total[...] += jnp.dot(features, rows, preferred_element_type=jnp.float32)
        return carry

    lax.fori_loop(0, CHUNKS, finish, 0)
    out_ref[...] = total[...].astype(jnp.bfloat16)

    def drain(i, carry):
        for copy in own_copies(i) + pass_copies(i):
            copy.wait_send()
        return carry

    lax.fori_loop(0, CHUNKS, drain, 0)
    outs.drain()


def block_rows(begin, end, ids, age, table, short_filter, mr_filter, mr_decay, columns, weight):
    vocab = table.shape[2]
    width = columns.shape[1]
    smem = pl.BlockSpec(memory_space=pltpu.SMEM)
    vmem = pl.BlockSpec(memory_space=pltpu.VMEM)
    return pl.pallas_call(
        block_kernel,
        out_shape=jax.ShapeDtypeStruct((ROWS, width), jnp.bfloat16),
        in_specs=[smem, smem] + [vmem] * 8,
        out_specs=vmem,
        scratch_shapes=[
            pltpu.VMEM((EXT, vocab), jnp.bfloat16),
            pltpu.VMEM((EXT, LANES), jnp.float32),
            pltpu.VMEM((EXT, LANES), jnp.float32),
            pltpu.VMEM((EXT + 8, 3 * LANES), jnp.float32),
            pltpu.VMEM((EXT, LANES), jnp.float32),
            pltpu.VMEM((TAPS, LANES), jnp.float32),
            pltpu.VMEM((R + 8, LANES), jnp.float32),
            pltpu.VMEM((TAPS, LANES), jnp.float32),
            pltpu.VMEM((ROWS, LANES), jnp.float32),
            pltpu.VMEM((SIDE, CHUNKS, ROWS, LANES), jnp.bfloat16),
            pltpu.VMEM((ROWS, width), jnp.float32),
            pltpu.VMEM((2 * PEERS, DEPTH // 2, width), jnp.bfloat16),
            pltpu.SemaphoreType.DMA((2, CHUNKS)),
            pltpu.SemaphoreType.DMA((2, CHUNKS)),
            pltpu.SemaphoreType.DMA((2, CHUNKS)),
            pltpu.SemaphoreType.DMA((2, CHUNKS)),
            pltpu.SemaphoreType.DMA((36,)),
            pltpu.SemaphoreType.DMA((36,)),
            pltpu.SemaphoreType.DMA((2,)),
        ],
        compiler_params=pltpu.CompilerParams(
            collective_id=1, has_side_effects=True, vmem_limit_bytes=56 * 2**20
        ),
        cost_estimate=pl.CostEstimate(flops=2 * ROWS * width * 4096, bytes_accessed=2**24, transcendentals=0),
    )(begin, end, ids, age, table, short_filter, mr_filter, mr_decay, columns, weight)


def body(
    token_ids,
    subst_pos,
    subst_base,
    window_lengths,
    embed_table,
    norm_gain,
    in_weight,
    short_filter,
    mr_filter,
    mr_decay,
    out_weight,
):
    row_count = token_ids.shape[0]
    vocab = embed_table.shape[0]
    width = out_weight.shape[1]

    matches = subst_pos[:, None] == jnp.arange(row_count, dtype=jnp.int32)[None, :]
    chosen = jnp.sum(jnp.where(matches, subst_base[:, None], 0), axis=0)
    touched = jnp.any(matches, axis=0)
    new_ids = jnp.where(touched, chosen, token_ids)

    shares = in_weight.reshape(DEPTH, 3, CHUNKS, LANES).transpose(2, 1, 3, 0).reshape(PEERS, 2, SHARE, DEPTH)
    shares = lax.dynamic_index_in_dim(shares, lax.axis_index("dp"), 1, keepdims=False)
    table, before = token_table(shares, embed_table, norm_gain[None, :], new_ids.reshape(-1, LANES))
    ids = jnp.concatenate([before.reshape(-1)[row_count - HALO :], new_ids])

    first_row = lax.axis_index("context") * row_count - HALO
    ends = jnp.cumsum(window_lengths)
    starts = ends - window_lengths
    positions = first_row + jnp.arange(EXT, dtype=jnp.int32)
    begins = jnp.max(jnp.where(starts[None, :] <= positions[:, None], starts[None, :], -1), axis=1)
    age = jnp.where(begins >= 0, positions - begins, -1)
    heads = first_row + HALO + R * jnp.arange(PIECES, dtype=jnp.int32)
    head_begin = jnp.max(jnp.where(starts[None, :] <= heads[:, None], starts[None, :], -1), axis=1)
    head_end = jnp.min(jnp.where(ends[None, :] > heads[:, None], ends[None, :], 1 << 20), axis=1)

    columns = lax.dynamic_slice_in_dim(embed_table, lax.axis_index("tensor") * width, width, 1)
    return block_rows(
        head_begin - first_row,
        head_end - first_row,
        ids[:, None],
        age[:, None],
        table,
        short_filter.reshape(3, 3, CHUNKS, LANES).transpose(2, 0, 1, 3),
        mr_filter.reshape(TAPS, CHUNKS, LANES).transpose(1, 0, 2),
        mr_decay.reshape(CHUNKS, 1, LANES),
        columns,
        out_weight.reshape(2, DEPTH // 2, width),
    )


def solution(mesh):
    in_specs = (
        P(("dp", "context")),
        P(("dp", "context")),
        P(("dp", "context")),
        P("dp"),
        P(),
        P(),
        P("context", None, "tensor"),
        P(None, None, "tensor"),
        P(None, "tensor"),
        P("tensor"),
        P("context", "tensor"),
    )
    out_specs = P(("dp", "context"), "tensor")
    return jax.shard_map(body, mesh=mesh, in_specs=in_specs, out_specs=out_specs, check_vma=False)
```

```python
import jax
import jax.numpy as jnp
from jax import lax
from jax.experimental import pallas as pl
from jax.experimental.pallas import tpu as pltpu
from jax.sharding import PartitionSpec as P

ROWS = 768
HALO = 144
EXT = HALO + ROWS
TAPS = 128
LANES = 128
R = 32
PIECES = ROWS // R
GROUP = 4
DEPTH = 256
SIDE = 4
PEERS = SIDE * SIDE
CHUNKS = 8
SHARE = 3 * LANES * CHUNKS // (2 * PEERS)
HALF = ROWS // 2
MESH = pl.DeviceIdType.MESH


def moved(c, k, sign):
    x = lax.rem(c // SIDE + SIDE + sign * (k // SIDE), SIDE)
    z = lax.rem(lax.rem(c, SIDE) + SIDE + sign * (k % SIDE), SIDE)
    return x * SIDE + z


def greet(axis_targets):
    barrier = pltpu.get_barrier_semaphore()
    for target in axis_targets:
        pl.semaphore_signal(barrier, inc=1, device_id=target, device_id_type=MESH)
    pl.semaphore_wait(barrier, len(axis_targets))


def send(source, target, sent, arrived, where):
    return pltpu.make_async_remote_copy(
        src_ref=source, dst_ref=target, send_sem=sent, recv_sem=arrived, device_id=where, device_id_type=MESH
    )


class Ring:
    def __init__(self, buffer, low, rows, sent, come):
        d = lax.axis_index("dp")
        c = lax.axis_index("context")
        self.x, self.z, self.d = c // SIDE, lax.rem(c, SIDE), d
        self.buffer, self.sent, self.come = buffer, sent, come
        self.low, self.high = pl.ds(0, low), pl.ds(low, rows - low)

    def context(self, j, m):
        dx = (1 - self.d) * m + self.d * j
        dz = (1 - self.d) * j + self.d * m
        return lax.rem(self.x + dx, SIDE) * SIDE + lax.rem(self.z + dz, SIDE)

    def copy(self, j, m, part, index, where):
        at = 2 * self.context(j, m) + self.d
        slot = self.buffer.at[at] if part is None else self.buffer.at[at, part]
        return send(slot, slot, self.sent.at[index], self.come.at[index], where)

    def along_a(self, side):
        return {"context": self.context(3 if side else 1, 0)}

    def along_b(self, side):
        return {"context": self.context(0, 3 if side else 1)}

    def first(self, side):
        return self.copy(0, 0, None, side, self.along_a(side))

    def second(self, side):
        return self.copy(1 if side else 3, 0, self.high if side else self.low, 2 + side, self.along_a(side))

    def third(self, j, side):
        return self.copy(j, 0, None, 4 + 2 * j + side, self.along_b(side))

    def fourth(self, j, side):
        return self.copy(
            j, 1 if side else 3, self.high if side else self.low, 12 + 2 * j + side, self.along_b(side)
        )

    def across(self, j, m):
        return self.copy(j, m, None, 20 + 4 * j + m, {"dp": 1 - self.d})

    def cross(self, *slots):
        for j, m in slots:
            self.across(j, m).start()

    def crossed(self, *slots):
        for j, m in slots:
            self.across(j, m).wait_recv()

    def hop1(self):
        for side in range(2):
            self.first(side).start()
            self.third(0, side).start()

    def hop2(self):
        for side in range(2):
            self.first(side).wait_recv()
            self.second(side).start()
            self.third(0, side).wait_recv()
            self.fourth(0, side).start()
        self.cross(*self.set2)
        for j in (1, 3):
            for side in range(2):
                self.third(j, side).start()

    def hop3(self):
        for side in range(2):
            self.second(side).wait_recv()
        for side in range(2):
            self.third(2, side).start()
        for side in range(2):
            self.fourth(0, side).wait_recv()
        for j in (1, 3):
            for side in range(2):
                self.third(j, side).wait_recv()
                self.fourth(j, side).start()
        self.cross(*self.set3)

    def hop4(self):
        for side in range(2):
            self.third(2, side).wait_recv()
            self.fourth(2, side).start()
        for j in (1, 3):
            for side in range(2):
                self.fourth(j, side).wait_recv()
        self.cross(*self.set4)

    def hop5(self):
        for side in range(2):
            self.fourth(2, side).wait_recv()
        self.cross(*self.set5)

    set2 = ((1, 0), (3, 0), (0, 1), (0, 3))
    set3 = ((2, 0), (0, 2), (1, 1), (1, 3), (3, 1), (3, 3))
    set4 = ((2, 1), (2, 3), (1, 2), (3, 2))
    set5 = ((2, 2),)

    def drain(self):
        for side in range(2):
            self.first(side).wait_send()
            self.second(side).wait_send()
            for j in range(SIDE):
                self.third(j, side).wait_send()
                self.fourth(j, side).wait_send()
        for j, m in self.set2 + self.set3 + self.set4 + self.set5:
            self.across(j, m).wait_send()


def table_kernel(
    shares,
    embed,
    gain,
    ids,
    table,
    before,
    got,
    normed,
    piece,
    sent_w,
    come_w,
    sent_t,
    come_t,
    ids_sem,
    local_sem,
):
    d = lax.axis_index("dp")
    c = lax.axis_index("context")
    other = {"dp": 1 - d}
    following = lax.rem(c + 1, PEERS)
    previous = lax.rem(c + PEERS - 1, PEERS)
    greet(
        [{"context": moved(c, k, 1)} for k in range(1, PEERS)]
        + [other, {"context": following}, {"context": previous}]
    )
    weights = [
        send(shares.at[moved(c, k, 1)], got.at[c], sent_w.at[k], come_w.at[k], {"context": moved(c, k, 1)})
        for k in range(1, PEERS)
    ]
    for copy in weights:
        copy.start()
    ids_copy = send(ids, before, ids_sem.at[0], ids_sem.at[1], {"context": following})
    ids_copy.start()

    vocab, width = embed.shape
    step = 32

    def norm_rows(i, carry):
        rows = pl.ds(pl.multiple_of(i * step, step), step)
        wide = embed[rows, :].astype(jnp.float32)
        scale = lax.rsqrt(jnp.mean(wide * wide, axis=1, keepdims=True) + 1e-06)
        values = (wide * scale * gain[...]).astype(jnp.bfloat16)
        for s in range(PEERS):
            normed[s, rows, :] = values[:, s * DEPTH : (s + 1) * DEPTH]
        return carry

    lax.fori_loop(0, vocab // step, norm_rows, 0)

    def product(weight, s):
        return lax.dot_general(
            weight, normed[s], (((1,), (1,)), ((), ())), preferred_element_type=jnp.float32
        )

    total = product(shares[c], c)
    for k in range(1, PEERS):
        weights[k - 1].wait_recv()
        origin = moved(c, k, -1)
        total = total + product(got[origin], origin)
    piece[...] = total.astype(jnp.bfloat16)
    local = pltpu.make_async_copy(piece, table.at[2 * c + d], local_sem)
    local.start()
    local.wait()
    ring = Ring(table, SHARE * 2 // 3, SHARE, sent_t, come_t)
    ring.hop1()
    ring.cross((0, 0))
    ring.hop2()
    ring.hop3()
    ring.hop4()
    ring.hop5()
    ring.crossed((0, 0), *Ring.set2, *Ring.set3, *Ring.set4, *Ring.set5)
    for copy in weights:
        copy.wait_send()
    ring.across(0, 0).wait_send()
    ring.drain()
    ids_copy.wait()


def token_table(shares, embed, gain, ids):
    vmem = pl.BlockSpec(memory_space=pltpu.VMEM)
    anywhere = pl.BlockSpec(memory_space=pl.ANY)
    vocab, width = embed.shape
    semaphores = [pltpu.SemaphoreType.DMA((PEERS,))] * 2 + [pltpu.SemaphoreType.DMA((36,))] * 2
    return pl.pallas_call(
        table_kernel,
        out_shape=(
            jax.ShapeDtypeStruct((2 * PEERS, SHARE, vocab), jnp.bfloat16),
            jax.ShapeDtypeStruct(ids.shape, jnp.int32),
        ),
        in_specs=[vmem, vmem, vmem, anywhere],
        out_specs=(anywhere, anywhere),
        scratch_shapes=[
            pltpu.VMEM((PEERS, SHARE, DEPTH), jnp.bfloat16),
            pltpu.VMEM((PEERS, vocab, DEPTH), jnp.bfloat16),
            pltpu.VMEM((SHARE, vocab), jnp.bfloat16),
            *semaphores,
            pltpu.SemaphoreType.DMA((2,)),
            pltpu.SemaphoreType.DMA,
        ],
        compiler_params=pltpu.CompilerParams(
            collective_id=0, has_side_effects=True, vmem_limit_bytes=40 * 2**20
        ),
        cost_estimate=pl.CostEstimate(flops=2 * SHARE * vocab * width, bytes_accessed=2**24, transcendentals=0),
    )(shares, embed, gain, ids)


def block_kernel(
    begin_ref,
    end_ref,
    ids_ref,
    age_ref,
    table,
    short_ref,
    filt_ref,
    decay_ref,
    columns,
    weight,
    out_ref,
    onehot,
    mask1,
    mask2,
    src,
    prod,
    window,
    recent,
    taps,
    longs,
    gates,
    total,
    weights,
    sent_own,
    come_own,
    sent_pass,
    come_pass,
    sent_w,
    come_w,
    local_sem,
):
    d = lax.axis_index("dp")
    c = lax.axis_index("context")
    t = lax.axis_index("tensor")
    right = lax.rem(t + 1, SIDE)
    left = lax.rem(t + SIDE - 1, SIDE)
    other = {"dp": 1 - d}
    greet(
        [{"tensor": right}, {"tensor": left}, other]
        + [{"context": moved(c, k, 1)} for k in range(1, PEERS)]
    )
    local = [pltpu.make_async_copy(weight.at[h], weights.at[2 * c + h], local_sem.at[h]) for h in range(2)]
    for copy in local:
        copy.start()
    outs = Ring(weights, LANES // 2, LANES, sent_w, come_w)

    vocab = onehot.shape[1]
    ids = jnp.broadcast_to(ids_ref[...], (EXT, vocab))
    onehot[...] = jnp.where(ids == lax.broadcasted_iota(jnp.int32, (EXT, vocab), 1), 1.0, 0.0).astype(jnp.bfloat16)
    age = jnp.broadcast_to(age_ref[...], (EXT, LANES))
    mask1[...] = (age >= 1).astype(jnp.float32)
    mask2[...] = (age >= 2).astype(jnp.float32)
    src[0:8, :] = jnp.zeros((8, 3 * LANES), jnp.float32)
    for copy in local:
        copy.wait()
    outs.hop1()

    def own_copies(i):
        return (
            send(gates.at[t, i], gates.at[t, i], sent_own.at[0, i], come_own.at[0, i], {"tensor": right}),
            send(gates.at[t, i], gates.at[t, i], sent_own.at[1, i], come_own.at[1, i], {"tensor": left}),
        )

    def pass_copies(i):
        low = (i, pl.ds(0, HALF))
        high = (i, pl.ds(HALF, HALF))
        return (
            send(gates.at[left, *low], gates.at[left, *low], sent_pass.at[0, i], come_pass.at[0, i], {"tensor": right}),
            send(gates.at[right, *high], gates.at[right, *high], sent_pass.at[1, i], come_pass.at[1, i], {"tensor": left}),
        )

    def hand_on(i):
        own, further = own_copies(i), pass_copies(i)
        for direction in range(2):
            own[direction].wait_recv()
            further[direction].start()

    def chunk(i, carry):
        for at, hop in ((1, outs.hop2), (3, outs.hop3), (5, outs.hop4), (6, outs.hop5)):
            pl.when(i == at)(hop)

        pieces = table[pl.ds(i * 4, 4)].reshape(3 * LANES, vocab)
        src[8:, :] = lax.dot_general(
            onehot[...], pieces, (((1,), (1,)), ((), ())), preferred_element_type=jnp.float32
        )
        tap_index = lax.broadcasted_iota(jnp.int32, (TAPS, LANES), 0).astype(jnp.float32)
        channels = pl.ds(pl.multiple_of(i * LANES, LANES), LANES)
        taps[...] = filt_ref[:, channels] * jnp.exp(-decay_ref[:, channels] * tap_index)
        filters = short_ref[:, :, channels]

        def mixed(g, low, count):
            lanes = slice(g * LANES, (g + 1) * LANES)
            return (
                filters[0, g : g + 1] * src[pl.ds(8 + low, count), lanes]
                + filters[1, g : g + 1] * (src[pl.ds(7 + low, count), lanes] * mask1[pl.ds(low, count), :])
                + filters[2, g : g + 1] * (src[pl.ds(6 + low, count), lanes] * mask2[pl.ds(low, count), :])
            )

        for low in range(0, EXT, 48):
            product = mixed(1, low, 48) * mixed(2, low, 48)
            prod[pl.ds(low, 48), :] = product.astype(jnp.bfloat16).astype(jnp.float32)

        def piece(n, carry):
            row = pl.multiple_of(HALO + n * R, 16)
            begin = begin_ref[n]
            end = end_ref[n]
            before = row - TAPS + lax.broadcasted_iota(jnp.int32, (TAPS, LANES), 0)
            window[...] = jnp.where(before >= begin, prod[pl.ds(row - TAPS, TAPS), :], 0.0)
            recent[...] = prod[pl.ds(row - 8, R + 8), :]
            age = jnp.broadcast_to(age_ref[pl.ds(row, R), :], (R, LANES))
            sums = [jnp.zeros((8, LANES), jnp.float32) for _ in range(R // 8)]
            near = [jnp.zeros((8, LANES), jnp.float32) for _ in range(R // 8)]
            for phase in range(8):
                for block in range(0, TAPS // 8, GROUP):
                    held = [
                        jnp.broadcast_to(taps[pl.ds(phase + 8 * (block + m), 1), :], (8, LANES))
                        for m in range(GROUP)
                    ]
                    views = {
                        q: window[pl.ds(TAPS + 8 * q - phase, 8), :]
                        if q < 0
                        else recent[pl.ds(8 + 8 * q - phase, 8), :]
                        for q in range(-(block + GROUP - 1), R // 8 - block)
                    }
                    for i in range(R // 8):
                        for m in range(GROUP):
                            q = i - block - m
                            if q < 0:
                                sums[i] = sums[i] + held[m] * views[q]
                            else:
                                kept = age[8 * i : 8 * i + 8] >= phase + 8 * (block + m)
                                near[i] = near[i] + held[m] * jnp.where(kept, views[q], 0.0)
            mine = row + lax.broadcasted_iota(jnp.int32, (R, LANES), 0) < end
            result = jnp.where(mine, jnp.concatenate(sums, axis=0), 0.0) + jnp.concatenate(near, axis=0)
            longs[pl.ds(pl.multiple_of(n * R, R), R), :] = result
            return carry

        lax.fori_loop(0, PIECES, piece, 0)
        for low in range(0, ROWS, 48):
            gated = mixed(0, HALO + low, 48) * longs[pl.ds(low, 48), :]
            gates[t, i, pl.ds(low, 48), :] = gated.astype(jnp.bfloat16)
        for copy in own_copies(i):
            copy.start()

        @pl.when(i > 0)
        def _():
            hand_on(i - 1)

        return carry

    lax.fori_loop(0, CHUNKS, chunk, 0)

    total[...] = jnp.dot(onehot[HALO:, :], columns[...], preferred_element_type=jnp.float32)
    outs.crossed(*Ring.set2, *Ring.set3, *Ring.set4, *Ring.set5)

    def finish(i, carry):
        for copy in pass_copies(i):
            copy.wait_recv()
        features = jnp.concatenate([gates[s, i] for s in range(SIDE)], axis=1)
        rows = jnp.concatenate([weights[s * CHUNKS + i] for s in range(SIDE)], axis=0)
        total[...] += jnp.dot(features, rows, preferred_element_type=jnp.float32)
        return carry

    lax.fori_loop(0, CHUNKS // 2, finish, 0)
    hand_on(CHUNKS - 1)
    lax.fori_loop(CHUNKS // 2, CHUNKS, finish, 0)
    out_ref[...] = total[...].astype(jnp.bfloat16)

    def drain(i, carry):
        for copy in own_copies(i) + pass_copies(i):
            copy.wait_send()
        return carry

    lax.fori_loop(0, CHUNKS, drain, 0)
    outs.drain()


def block_rows(begin, end, ids, age, table, short_filter, mr_filter, mr_decay, columns, weight):
    vocab = table.shape[2]
    width = columns.shape[1]
    smem = pl.BlockSpec(memory_space=pltpu.SMEM)
    vmem = pl.BlockSpec(memory_space=pltpu.VMEM)
    return pl.pallas_call(
        block_kernel,
        out_shape=jax.ShapeDtypeStruct((ROWS, width), jnp.bfloat16),
        in_specs=[smem, smem] + [vmem] * 8,
        out_specs=vmem,
        scratch_shapes=[
            pltpu.VMEM((EXT, vocab), jnp.bfloat16),
            pltpu.VMEM((EXT, LANES), jnp.float32),
            pltpu.VMEM((EXT, LANES), jnp.float32),
            pltpu.VMEM((EXT + 8, 3 * LANES), jnp.float32),
            pltpu.VMEM((EXT, LANES), jnp.float32),
            pltpu.VMEM((TAPS, LANES), jnp.float32),
            pltpu.VMEM((R + 8, LANES), jnp.float32),
            pltpu.VMEM((TAPS, LANES), jnp.float32),
            pltpu.VMEM((ROWS, LANES), jnp.float32),
            pltpu.VMEM((SIDE, CHUNKS, ROWS, LANES), jnp.bfloat16),
            pltpu.VMEM((ROWS, width), jnp.float32),
            pltpu.VMEM((2 * PEERS, DEPTH // 2, width), jnp.bfloat16),
            pltpu.SemaphoreType.DMA((2, CHUNKS)),
            pltpu.SemaphoreType.DMA((2, CHUNKS)),
            pltpu.SemaphoreType.DMA((2, CHUNKS)),
            pltpu.SemaphoreType.DMA((2, CHUNKS)),
            pltpu.SemaphoreType.DMA((36,)),
            pltpu.SemaphoreType.DMA((36,)),
            pltpu.SemaphoreType.DMA((2,)),
        ],
        compiler_params=pltpu.CompilerParams(
            collective_id=1, has_side_effects=True, vmem_limit_bytes=56 * 2**20
        ),
        cost_estimate=pl.CostEstimate(flops=2 * ROWS * width * 4096, bytes_accessed=2**24, transcendentals=0),
    )(begin, end, ids, age, table, short_filter, mr_filter, mr_decay, columns, weight)


def body(
    token_ids,
    subst_pos,
    subst_base,
    window_lengths,
    embed_table,
    norm_gain,
    in_weight,
    short_filter,
    mr_filter,
    mr_decay,
    out_weight,
):
    row_count = token_ids.shape[0]
    vocab = embed_table.shape[0]
    width = out_weight.shape[1]

    matches = subst_pos[:, None] == jnp.arange(row_count, dtype=jnp.int32)[None, :]
    chosen = jnp.sum(jnp.where(matches, subst_base[:, None], 0), axis=0)
    touched = jnp.any(matches, axis=0)
    new_ids = jnp.where(touched, chosen, token_ids)

    shares = in_weight.reshape(DEPTH, 3, CHUNKS, LANES).transpose(2, 1, 3, 0).reshape(PEERS, 2, SHARE, DEPTH)
    shares = lax.dynamic_index_in_dim(shares, lax.axis_index("dp"), 1, keepdims=False)
    table, before = token_table(shares, embed_table, norm_gain[None, :], new_ids.reshape(-1, LANES))
    ids = jnp.concatenate([before.reshape(-1)[row_count - HALO :], new_ids])

    first_row = lax.axis_index("context") * row_count - HALO
    ends = jnp.cumsum(window_lengths)
    starts = ends - window_lengths
    positions = first_row + jnp.arange(EXT, dtype=jnp.int32)
    begins = jnp.max(jnp.where(starts[None, :] <= positions[:, None], starts[None, :], -1), axis=1)
    age = jnp.where(begins >= 0, positions - begins, -1)
    heads = first_row + HALO + R * jnp.arange(PIECES, dtype=jnp.int32)
    head_begin = jnp.max(jnp.where(starts[None, :] <= heads[:, None], starts[None, :], -1), axis=1)
    head_end = jnp.min(jnp.where(ends[None, :] > heads[:, None], ends[None, :], 1 << 20), axis=1)

    columns = lax.dynamic_slice_in_dim(embed_table, lax.axis_index("tensor") * width, width, 1)
    return block_rows(
        head_begin - first_row,
        head_end - first_row,
        ids[:, None],
        age[:, None],
        table,
        short_filter,
        mr_filter,
        mr_decay[None, :],
        columns,
        out_weight.reshape(2, DEPTH // 2, width),
    )


def solution(mesh):
    in_specs = (
        P(("dp", "context")),
        P(("dp", "context")),
        P(("dp", "context")),
        P("dp"),
        P(),
        P(),
        P("context", None, "tensor"),
        P(None, None, "tensor"),
        P(None, "tensor"),
        P("tensor"),
        P("context", "tensor"),
    )
    out_specs = P(("dp", "context"), "tensor")
    return jax.shard_map(body, mesh=mesh, in_specs=in_specs, out_specs=out_specs, check_vma=False)
```

```python
import jax
import jax.numpy as jnp
from jax import lax
from jax.experimental import pallas as pl
from jax.experimental.pallas import tpu as pltpu
from jax.sharding import PartitionSpec as P

ROWS = 768
HALO = 144
EXT = HALO + ROWS
TAPS = 128
LANES = 128
R = 32
PIECES = ROWS // R
GROUP = 4
DEPTH = 256
SIDE = 4
PEERS = SIDE * SIDE
CHUNKS = 8
SHARE = 3 * LANES * CHUNKS // (2 * PEERS)
HALF = ROWS // 2
MESH = pl.DeviceIdType.MESH


def moved(c, k, sign):
    x = lax.rem(c // SIDE + SIDE + sign * (k // SIDE), SIDE)
    z = lax.rem(lax.rem(c, SIDE) + SIDE + sign * (k % SIDE), SIDE)
    return x * SIDE + z


def tree_sum(terms):
    while len(terms) > 1:
        terms = [sum(terms[k + 1 : k + 2], terms[k]) for k in range(0, len(terms), 2)]
    return terms[0]


def greet(axis_targets):
    barrier = pltpu.get_barrier_semaphore()
    for target in axis_targets:
        pl.semaphore_signal(barrier, inc=1, device_id=target, device_id_type=MESH)
    pl.semaphore_wait(barrier, len(axis_targets))


def send(source, target, sent, arrived, where):
    return pltpu.make_async_remote_copy(
        src_ref=source, dst_ref=target, send_sem=sent, recv_sem=arrived, device_id=where, device_id_type=MESH
    )


class Ring:
    def __init__(self, buffer, low, rows, sent, come):
        d = lax.axis_index("dp")
        c = lax.axis_index("context")
        self.x, self.z, self.d = c // SIDE, lax.rem(c, SIDE), d
        self.buffer, self.sent, self.come = buffer, sent, come
        self.low, self.high = pl.ds(0, low), pl.ds(low, rows - low)

    def context(self, j, m):
        dx = (1 - self.d) * m + self.d * j
        dz = (1 - self.d) * j + self.d * m
        return lax.rem(self.x + dx, SIDE) * SIDE + lax.rem(self.z + dz, SIDE)

    def copy(self, j, m, part, index, where):
        at = 2 * self.context(j, m) + self.d
        slot = self.buffer.at[at] if part is None else self.buffer.at[at, part]
        return send(slot, slot, self.sent.at[index], self.come.at[index], where)

    def along_a(self, side):
        return {"context": self.context(3 if side else 1, 0)}

    def along_b(self, side):
        return {"context": self.context(0, 3 if side else 1)}

    def first(self, side):
        return self.copy(0, 0, None, side, self.along_a(side))

    def second(self, side):
        return self.copy(1 if side else 3, 0, self.high if side else self.low, 2 + side, self.along_a(side))

    def third(self, j, side):
        return self.copy(j, 0, None, 4 + 2 * j + side, self.along_b(side))

    def fourth(self, j, side):
        return self.copy(
            j, 1 if side else 3, self.high if side else self.low, 12 + 2 * j + side, self.along_b(side)
        )

    def across(self, j, m):
        return self.copy(j, m, None, 20 + 4 * j + m, {"dp": 1 - self.d})

    def cross(self, *slots):
        for j, m in slots:
            self.across(j, m).start()

    def crossed(self, *slots):
        for j, m in slots:
            self.across(j, m).wait_recv()

    def hop1(self):
        for side in range(2):
            self.first(side).start()
            self.third(0, side).start()

    def hop2(self):
        for side in range(2):
            self.first(side).wait_recv()
            self.second(side).start()
            self.third(0, side).wait_recv()
            self.fourth(0, side).start()
        self.cross(*self.set2)
        for j in (1, 3):
            for side in range(2):
                self.third(j, side).start()

    def hop3(self):
        for side in range(2):
            self.second(side).wait_recv()
        for side in range(2):
            self.third(2, side).start()
        for side in range(2):
            self.fourth(0, side).wait_recv()
        for j in (1, 3):
            for side in range(2):
                self.third(j, side).wait_recv()
                self.fourth(j, side).start()
        self.cross(*self.set3)

    def hop4(self):
        for side in range(2):
            self.third(2, side).wait_recv()
            self.fourth(2, side).start()
        for j in (1, 3):
            for side in range(2):
                self.fourth(j, side).wait_recv()
        self.cross(*self.set4)

    def hop5(self):
        for side in range(2):
            self.fourth(2, side).wait_recv()
        self.cross(*self.set5)

    set2 = ((1, 0), (3, 0), (0, 1), (0, 3))
    set3 = ((2, 0), (0, 2), (1, 1), (1, 3), (3, 1), (3, 3))
    set4 = ((2, 1), (2, 3), (1, 2), (3, 2))
    set5 = ((2, 2),)

    def drain(self):
        for side in range(2):
            self.first(side).wait_send()
            self.second(side).wait_send()
            for j in range(SIDE):
                self.third(j, side).wait_send()
                self.fourth(j, side).wait_send()
        for j, m in self.set2 + self.set3 + self.set4 + self.set5:
            self.across(j, m).wait_send()


def table_kernel(
    shares,
    embed,
    gain,
    ids,
    table,
    before,
    columns,
    got,
    wide,
    normed,
    piece,
    sent_w,
    come_w,
    sent_t,
    come_t,
    ids_sem,
    local_sem,
    embed_sem,
):
    d = lax.axis_index("dp")
    c = lax.axis_index("context")
    local_embed = pltpu.make_async_copy(embed, wide, embed_sem)
    local_embed.start()
    other = {"dp": 1 - d}
    following = lax.rem(c + 1, PEERS)
    previous = lax.rem(c + PEERS - 1, PEERS)
    greet(
        [{"context": moved(c, k, 1)} for k in range(1, PEERS)]
        + [other, {"context": following}, {"context": previous}]
    )
    weights = [
        send(shares.at[moved(c, k, 1)], got.at[c], sent_w.at[k], come_w.at[k], {"context": moved(c, k, 1)})
        for k in range(1, PEERS)
    ]
    for copy in weights:
        copy.start()
    ids_copy = send(ids, before, ids_sem.at[0], ids_sem.at[1], {"context": following})
    ids_copy.start()

    local_embed.wait()
    vocab, width = embed.shape
    step = 32

    def norm_rows(i, carry):
        rows = pl.ds(pl.multiple_of(i * step, step), step)
        values = wide[rows, :].astype(jnp.float32)
        scale = lax.rsqrt(jnp.mean(values * values, axis=1, keepdims=True) + 1e-06)
        values = (values * scale * gain[...]).astype(jnp.bfloat16)
        for s in range(PEERS):
            normed[s, rows, :] = values[:, s * DEPTH : (s + 1) * DEPTH]
        return carry

    lax.fori_loop(0, vocab // step, norm_rows, 0)

    own = pl.ds(pl.multiple_of(lax.axis_index("tensor") * columns.shape[1], LANES), columns.shape[1])
    columns[...] = wide[:, own]

    def product(weight, s):
        return lax.dot_general(
            weight, normed[s], (((1,), (1,)), ((), ())), preferred_element_type=jnp.float32
        )

    total = product(shares[c], c)
    for k in range(1, PEERS):
        weights[k - 1].wait_recv()
        origin = moved(c, k, -1)
        total = total + product(got[origin], origin)
    piece[...] = total.astype(jnp.bfloat16)
    local = pltpu.make_async_copy(piece, table.at[2 * c + d], local_sem)
    local.start()
    local.wait()
    ring = Ring(table, SHARE * 2 // 3, SHARE, sent_t, come_t)
    ring.hop1()
    ring.cross((0, 0))
    ring.hop2()
    ring.hop3()
    ring.hop4()
    ring.hop5()
    ring.crossed((0, 0), *Ring.set2, *Ring.set3, *Ring.set4, *Ring.set5)
    for copy in weights:
        copy.wait_send()
    ring.across(0, 0).wait_send()
    ring.drain()
    ids_copy.wait()


def token_table(shares, embed, gain, ids):
    vmem = pl.BlockSpec(memory_space=pltpu.VMEM)
    anywhere = pl.BlockSpec(memory_space=pl.ANY)
    vocab, width = embed.shape
    semaphores = [pltpu.SemaphoreType.DMA((PEERS,))] * 2 + [pltpu.SemaphoreType.DMA((36,))] * 2
    return pl.pallas_call(
        table_kernel,
        out_shape=(
            jax.ShapeDtypeStruct((2 * PEERS, SHARE, vocab), jnp.bfloat16),
            jax.ShapeDtypeStruct(ids.shape, jnp.int32),
            jax.ShapeDtypeStruct((vocab, width // SIDE), jnp.bfloat16),
        ),
        in_specs=[vmem, anywhere, vmem, anywhere],
        out_specs=(anywhere, anywhere, vmem),
        scratch_shapes=[
            pltpu.VMEM((PEERS, SHARE, DEPTH), jnp.bfloat16),
            pltpu.VMEM((vocab, width), jnp.bfloat16),
            pltpu.VMEM((PEERS, vocab, DEPTH), jnp.bfloat16),
            pltpu.VMEM((SHARE, vocab), jnp.bfloat16),
            *semaphores,
            pltpu.SemaphoreType.DMA((2,)),
            pltpu.SemaphoreType.DMA,
            pltpu.SemaphoreType.DMA,
        ],
        compiler_params=pltpu.CompilerParams(
            collective_id=0, has_side_effects=True, vmem_limit_bytes=40 * 2**20
        ),
        cost_estimate=pl.CostEstimate(flops=2 * SHARE * vocab * width, bytes_accessed=2**24, transcendentals=0),
    )(shares, embed, gain, ids)


def block_kernel(
    ids_ref,
    age_ref,
    table_in,
    short_ref,
    filt_ref,
    decay_ref,
    columns,
    weight,
    out_ref,
    table,
    onehot,
    mask1,
    mask2,
    src,
    prod,
    window,
    recent,
    taps,
    longs,
    gates,
    total,
    weights,
    sent_own,
    come_own,
    sent_pass,
    come_pass,
    sent_w,
    come_w,
    local_sem,
):
    d = lax.axis_index("dp")
    c = lax.axis_index("context")
    t = lax.axis_index("tensor")
    right = lax.rem(t + 1, SIDE)
    left = lax.rem(t + SIDE - 1, SIDE)
    other = {"dp": 1 - d}
    local_table = pltpu.make_async_copy(table_in, table, local_sem.at[2])
    local_table.start()
    greet(
        [{"tensor": right}, {"tensor": left}, other]
        + [{"context": moved(c, k, 1)} for k in range(1, PEERS)]
    )
    local = [pltpu.make_async_copy(weight.at[h], weights.at[2 * c + h], local_sem.at[h]) for h in range(2)]
    for copy in local:
        copy.start()
    outs = Ring(weights, LANES // 2, LANES, sent_w, come_w)

    vocab = onehot.shape[1]
    ids = jnp.broadcast_to(ids_ref[...], (EXT, vocab))
    onehot[...] = jnp.where(ids == lax.broadcasted_iota(jnp.int32, (EXT, vocab), 1), 1.0, 0.0).astype(jnp.bfloat16)
    age = jnp.broadcast_to(age_ref[...], (EXT, LANES))
    mask1[...] = (age >= 1).astype(jnp.float32)
    mask2[...] = (age >= 2).astype(jnp.float32)
    src[0:8, :] = jnp.zeros((8, 3 * LANES), jnp.float32)
    for copy in local:
        copy.wait()
    outs.hop1()
    local_table.wait()

    def own_copies(i):
        return (
            send(gates.at[t, i], gates.at[t, i], sent_own.at[0, i], come_own.at[0, i], {"tensor": right}),
            send(gates.at[t, i], gates.at[t, i], sent_own.at[1, i], come_own.at[1, i], {"tensor": left}),
        )

    def pass_copies(i):
        low = (i, pl.ds(0, HALF))
        high = (i, pl.ds(HALF, HALF))
        return (
            send(gates.at[left, *low], gates.at[left, *low], sent_pass.at[0, i], come_pass.at[0, i], {"tensor": right}),
            send(gates.at[right, *high], gates.at[right, *high], sent_pass.at[1, i], come_pass.at[1, i], {"tensor": left}),
        )

    def hand_on(i):
        own, further = own_copies(i), pass_copies(i)
        for direction in range(2):
            own[direction].wait_recv()
            further[direction].start()

    def chunk(i, carry):
        for at, hop in ((1, outs.hop2), (3, outs.hop3), (5, outs.hop4), (6, outs.hop5)):
            pl.when(i == at)(hop)

        pieces = table[pl.ds(i * 4, 4)].reshape(3 * LANES, vocab)
        src[8:, :] = lax.dot_general(
            onehot[...], pieces, (((1,), (1,)), ((), ())), preferred_element_type=jnp.float32
        )
        tap_index = lax.broadcasted_iota(jnp.int32, (TAPS, LANES), 0).astype(jnp.float32)
        channels = pl.ds(pl.multiple_of(i * LANES, LANES), LANES)
        values = filt_ref[:, channels] * jnp.exp(-decay_ref[:, channels] * tap_index)
        for j in range(TAPS):
            taps[j] = jnp.broadcast_to(values[j : j + 1], (8, LANES))
        filters = short_ref[:, :, channels]

        def mixed(g, low, count):
            lanes = slice(g * LANES, (g + 1) * LANES)
            return (
                filters[0, g : g + 1] * src[pl.ds(8 + low, count), lanes]
                + filters[1, g : g + 1] * (src[pl.ds(7 + low, count), lanes] * mask1[pl.ds(low, count), :])
                + filters[2, g : g + 1] * (src[pl.ds(6 + low, count), lanes] * mask2[pl.ds(low, count), :])
            )

        for low in range(0, EXT, 48):
            product = mixed(1, low, 48) * mixed(2, low, 48)
            prod[pl.ds(low, 48), :] = product.astype(jnp.bfloat16).astype(jnp.float32)

        def piece(n, carry):
            row = pl.multiple_of(HALO + n * R, 16)
            head = row - jnp.broadcast_to(age_ref[pl.ds(row, 1), :], (TAPS, LANES))
            before = row - TAPS + lax.broadcasted_iota(jnp.int32, (TAPS, LANES), 0)
            window[...] = jnp.where(before >= head, prod[pl.ds(row - TAPS, TAPS), :], 0.0)
            recent[...] = prod[pl.ds(row - 8, R + 8), :]
            age = jnp.broadcast_to(age_ref[pl.ds(row, R), :], (R, LANES))
            sums = [jnp.zeros((8, LANES), jnp.float32) for _ in range(R // 8)]
            near = [jnp.zeros((8, LANES), jnp.float32) for _ in range(R // 8)]
            for phase in range(8):
                for block in range(0, TAPS // 8, GROUP):
                    held = [taps[phase + 8 * (block + m)] for m in range(GROUP)]
                    views = {
                        q: window[pl.ds(TAPS + 8 * q - phase, 8), :]
                        if q < 0
                        else recent[pl.ds(8 + 8 * q - phase, 8), :]
                        for q in range(-(block + GROUP - 1), R // 8 - block)
                    }
                    for i in range(R // 8):
                        far, close = [], []
                        for m in range(GROUP):
                            q = i - block - m
                            if q < 0:
                                far.append(held[m] * views[q])
                            else:
                                kept = age[8 * i : 8 * i + 8] >= phase + 8 * (block + m)
                                close.append(held[m] * jnp.where(kept, views[q], 0.0))
                        if far:
                            sums[i] = sums[i] + tree_sum(far)
                        if close:
                            near[i] = near[i] + tree_sum(close)
            mine = row + lax.broadcasted_iota(jnp.int32, (R, LANES), 0) - age == head[:R]
            result = jnp.where(mine, jnp.concatenate(sums, axis=0), 0.0) + jnp.concatenate(near, axis=0)
            longs[pl.ds(pl.multiple_of(n * R, R), R), :] = result
            return carry

        lax.fori_loop(0, PIECES, piece, 0)
        for low in range(0, ROWS, 48):
            gated = mixed(0, HALO + low, 48) * longs[pl.ds(low, 48), :]
            gates[t, i, pl.ds(low, 48), :] = gated.astype(jnp.bfloat16)
        for copy in own_copies(i):
            copy.start()

        @pl.when(i > 0)
        def _():
            hand_on(i - 1)

        return carry

    lax.fori_loop(0, CHUNKS, chunk, 0)

    total[...] = jnp.dot(onehot[HALO:, :], columns[...], preferred_element_type=jnp.float32)
    outs.crossed(*Ring.set2, *Ring.set3, *Ring.set4, *Ring.set5)

    def finish(i, carry):
        for copy in pass_copies(i):
            copy.wait_recv()
        features = jnp.concatenate([gates[s, i] for s in range(SIDE)], axis=1)
        rows = jnp.concatenate([weights[s * CHUNKS + i] for s in range(SIDE)], axis=0)
        total[...] += jnp.dot(features, rows, preferred_element_type=jnp.float32)
        return carry

    lax.fori_loop(0, CHUNKS // 2, finish, 0)
    hand_on(CHUNKS - 1)
    lax.fori_loop(CHUNKS // 2, CHUNKS, finish, 0)
    out_ref[...] = total[...].astype(jnp.bfloat16)

    def drain(i, carry):
        for copy in own_copies(i) + pass_copies(i):
            copy.wait_send()
        return carry

    lax.fori_loop(0, CHUNKS, drain, 0)
    outs.drain()


def block_rows(ids, age, table, short_filter, mr_filter, mr_decay, columns, weight):
    vocab = table.shape[2]
    width = columns.shape[1]
    vmem = pl.BlockSpec(memory_space=pltpu.VMEM)
    anywhere = pl.BlockSpec(memory_space=pl.ANY)
    return pl.pallas_call(
        block_kernel,
        out_shape=jax.ShapeDtypeStruct((ROWS, width), jnp.bfloat16),
        in_specs=[vmem] * 2 + [anywhere] + [vmem] * 4 + [anywhere],
        out_specs=vmem,
        scratch_shapes=[
            pltpu.VMEM(table.shape, jnp.bfloat16),
            pltpu.VMEM((EXT, vocab), jnp.bfloat16),
            pltpu.VMEM((EXT, LANES), jnp.float32),
            pltpu.VMEM((EXT, LANES), jnp.float32),
            pltpu.VMEM((EXT + 8, 3 * LANES), jnp.float32),
            pltpu.VMEM((EXT, LANES), jnp.float32),
            pltpu.VMEM((TAPS, LANES), jnp.float32),
            pltpu.VMEM((R + 8, LANES), jnp.float32),
            pltpu.VMEM((TAPS, 8, LANES), jnp.float32),
            pltpu.VMEM((ROWS, LANES), jnp.float32),
            pltpu.VMEM((SIDE, CHUNKS, ROWS, LANES), jnp.bfloat16),
            pltpu.VMEM((ROWS, width), jnp.float32),
            pltpu.VMEM((2 * PEERS, DEPTH // 2, width), jnp.bfloat16),
            pltpu.SemaphoreType.DMA((2, CHUNKS)),
            pltpu.SemaphoreType.DMA((2, CHUNKS)),
            pltpu.SemaphoreType.DMA((2, CHUNKS)),
            pltpu.SemaphoreType.DMA((2, CHUNKS)),
            pltpu.SemaphoreType.DMA((36,)),
            pltpu.SemaphoreType.DMA((36,)),
            pltpu.SemaphoreType.DMA((3,)),
        ],
        compiler_params=pltpu.CompilerParams(
            collective_id=1, has_side_effects=True, vmem_limit_bytes=56 * 2**20
        ),
        cost_estimate=pl.CostEstimate(flops=2 * ROWS * width * 4096, bytes_accessed=2**24, transcendentals=0),
    )(ids, age, table, short_filter, mr_filter, mr_decay, columns, weight)


def body(
    token_ids,
    subst_pos,
    subst_base,
    window_lengths,
    embed_table,
    norm_gain,
    in_weight,
    short_filter,
    mr_filter,
    mr_decay,
    out_weight,
):
    row_count = token_ids.shape[0]
    vocab = embed_table.shape[0]
    width = out_weight.shape[1]

    matches = subst_pos[:, None] == jnp.arange(row_count, dtype=jnp.int32)[None, :]
    chosen = jnp.max(jnp.where(matches, subst_base[:, None], -1), axis=0)
    new_ids = jnp.where(chosen >= 0, chosen, token_ids)

    shares = in_weight.reshape(DEPTH, 3, CHUNKS, LANES).transpose(2, 1, 3, 0).reshape(PEERS, 2, SHARE, DEPTH)
    shares = lax.dynamic_index_in_dim(shares, lax.axis_index("dp"), 1, keepdims=False)
    table, before, columns = token_table(shares, embed_table, norm_gain[None, :], new_ids.reshape(-1, LANES))
    ids = jnp.concatenate([before.reshape(-1)[row_count - HALO :], new_ids])

    first_row = lax.axis_index("context") * row_count - HALO
    windows = jnp.arange(window_lengths.shape[0], dtype=jnp.int32)
    starts = jnp.sum(jnp.where(windows[None, :] < windows[:, None], window_lengths[None, :], 0), axis=1)
    positions = first_row + jnp.arange(EXT, dtype=jnp.int32)
    begins = jnp.max(jnp.where(starts[None, :] <= positions[:, None], starts[None, :], -1), axis=1)
    age = jnp.where(begins >= 0, positions - begins, -1)
    return block_rows(
        ids[:, None],
        age[:, None],
        table,
        short_filter,
        mr_filter,
        mr_decay[None, :],
        columns,
        out_weight.reshape(2, DEPTH // 2, width),
    )


def solution(mesh):
    in_specs = (
        P(("dp", "context")),
        P(("dp", "context")),
        P(("dp", "context")),
        P("dp"),
        P(),
        P(),
        P("context", None, "tensor"),
        P(None, None, "tensor"),
        P(None, "tensor"),
        P("tensor"),
        P("context", "tensor"),
    )
    out_specs = P(("dp", "context"), "tensor")
    return jax.shard_map(body, mesh=mesh, in_specs=in_specs, out_specs=out_specs, check_vma=False)
```

```python
import jax
import jax.numpy as jnp
from jax import lax
from jax.experimental import pallas as pl
from jax.experimental.pallas import tpu as pltpu
from jax.sharding import PartitionSpec as P

ROWS = 768
HALO = 144
EXT = HALO + ROWS
TAPS = 128
LANES = 128
R = 32
PIECES = ROWS // R
GROUP = 4
DEPTH = 256
SIDE = 4
PEERS = SIDE * SIDE
CHUNKS = 8
SHARE = 3 * LANES * CHUNKS // (2 * PEERS)
HALF = ROWS // 2
MESH = pl.DeviceIdType.MESH


def moved(c, k, sign):
    x = lax.rem(c // SIDE + SIDE + sign * (k // SIDE), SIDE)
    z = lax.rem(lax.rem(c, SIDE) + SIDE + sign * (k % SIDE), SIDE)
    return x * SIDE + z


def tree_sum(terms):
    while len(terms) > 1:
        terms = [sum(terms[k + 1 : k + 2], terms[k]) for k in range(0, len(terms), 2)]
    return terms[0]


def greet(axis_targets):
    barrier = pltpu.get_barrier_semaphore()
    for target in axis_targets:
        pl.semaphore_signal(barrier, inc=1, device_id=target, device_id_type=MESH)
    pl.semaphore_wait(barrier, len(axis_targets))


def send(source, target, sent, arrived, where):
    return pltpu.make_async_remote_copy(
        src_ref=source, dst_ref=target, send_sem=sent, recv_sem=arrived, device_id=where, device_id_type=MESH
    )


class Ring:
    def __init__(self, buffer, low, rows, sent, come):
        d = lax.axis_index("dp")
        c = lax.axis_index("context")
        self.x, self.z, self.d = c // SIDE, lax.rem(c, SIDE), d
        self.buffer, self.sent, self.come = buffer, sent, come
        self.low, self.high = pl.ds(0, low), pl.ds(low, rows - low)

    def context(self, j, m):
        dx = (1 - self.d) * m + self.d * j
        dz = (1 - self.d) * j + self.d * m
        return lax.rem(self.x + dx, SIDE) * SIDE + lax.rem(self.z + dz, SIDE)

    def copy(self, j, m, part, index, where):
        at = 2 * self.context(j, m) + self.d
        slot = self.buffer.at[at] if part is None else self.buffer.at[at, part]
        return send(slot, slot, self.sent.at[index], self.come.at[index], where)

    def along_a(self, side):
        return {"context": self.context(3 if side else 1, 0)}

    def along_b(self, side):
        return {"context": self.context(0, 3 if side else 1)}

    def first(self, side):
        return self.copy(0, 0, None, side, self.along_a(side))

    def second(self, side):
        return self.copy(1 if side else 3, 0, self.high if side else self.low, 2 + side, self.along_a(side))

    def third(self, j, side):
        return self.copy(j, 0, None, 4 + 2 * j + side, self.along_b(side))

    def fourth(self, j, side):
        return self.copy(
            j, 1 if side else 3, self.high if side else self.low, 12 + 2 * j + side, self.along_b(side)
        )

    def across(self, j, m):
        return self.copy(j, m, None, 20 + 4 * j + m, {"dp": 1 - self.d})

    def cross(self, *slots):
        for j, m in slots:
            self.across(j, m).start()

    def crossed(self, *slots):
        for j, m in slots:
            self.across(j, m).wait_recv()

    def hop1(self):
        for side in range(2):
            self.first(side).start()
            self.third(0, side).start()

    def hop2(self):
        for side in range(2):
            self.first(side).wait_recv()
            self.second(side).start()
            self.third(0, side).wait_recv()
            self.fourth(0, side).start()
        self.cross(*self.set2)
        for j in (1, 3):
            for side in range(2):
                self.third(j, side).start()

    def hop3(self):
        for side in range(2):
            self.second(side).wait_recv()
        for side in range(2):
            self.third(2, side).start()
        for side in range(2):
            self.fourth(0, side).wait_recv()
        for j in (1, 3):
            for side in range(2):
                self.third(j, side).wait_recv()
                self.fourth(j, side).start()
        self.cross(*self.set3)

    def hop4(self):
        for side in range(2):
            self.third(2, side).wait_recv()
            self.fourth(2, side).start()
        for j in (1, 3):
            for side in range(2):
                self.fourth(j, side).wait_recv()
        self.cross(*self.set4)

    def hop5(self):
        for side in range(2):
            self.fourth(2, side).wait_recv()
        self.cross(*self.set5)

    set2 = ((1, 0), (3, 0), (0, 1), (0, 3))
    set3 = ((2, 0), (0, 2), (1, 1), (1, 3), (3, 1), (3, 3))
    set4 = ((2, 1), (2, 3), (1, 2), (3, 2))
    set5 = ((2, 2),)

    def drain(self):
        for side in range(2):
            self.first(side).wait_send()
            self.second(side).wait_send()
            for j in range(SIDE):
                self.third(j, side).wait_send()
                self.fourth(j, side).wait_send()
        for j, m in self.set2 + self.set3 + self.set4 + self.set5:
            self.across(j, m).wait_send()


def table_kernel(
    shares,
    embed,
    gain,
    ids,
    table,
    before,
    columns,
    got,
    wide,
    normed,
    piece,
    sent_w,
    come_w,
    sent_t,
    come_t,
    ids_sem,
    local_sem,
    embed_sem,
):
    d = lax.axis_index("dp")
    c = lax.axis_index("context")
    local_embed = pltpu.make_async_copy(embed, wide, embed_sem)
    local_embed.start()
    other = {"dp": 1 - d}
    following = lax.rem(c + 1, PEERS)
    previous = lax.rem(c + PEERS - 1, PEERS)
    greet(
        [{"context": moved(c, k, 1)} for k in range(1, PEERS)]
        + [other, {"context": following}, {"context": previous}]
    )
    weights = [
        send(shares.at[moved(c, k, 1)], got.at[c], sent_w.at[k], come_w.at[k], {"context": moved(c, k, 1)})
        for k in range(1, PEERS)
    ]
    for copy in weights:
        copy.start()
    ids_copy = send(ids, before, ids_sem.at[0], ids_sem.at[1], {"context": following})
    ids_copy.start()

    local_embed.wait()
    vocab, width = embed.shape
    step = 32

    def norm_rows(i, carry):
        rows = pl.ds(pl.multiple_of(i * step, step), step)
        values = wide[rows, :].astype(jnp.float32)
        scale = lax.rsqrt(jnp.mean(values * values, axis=1, keepdims=True) + 1e-06)
        values = (values * scale * gain[...]).astype(jnp.bfloat16)
        for s in range(PEERS):
            normed[s, rows, :] = values[:, s * DEPTH : (s + 1) * DEPTH]
        return carry

    lax.fori_loop(0, vocab // step, norm_rows, 0)

    own = pl.ds(pl.multiple_of(lax.axis_index("tensor") * columns.shape[1], LANES), columns.shape[1])
    columns[...] = wide[:, own]

    def product(weight, s):
        return lax.dot_general(
            weight, normed[s], (((1,), (1,)), ((), ())), preferred_element_type=jnp.float32
        )

    total = product(shares[c], c)
    for k in range(1, PEERS):
        weights[k - 1].wait_recv()
        origin = moved(c, k, -1)
        total = total + product(got[origin], origin)
    piece[...] = total.astype(jnp.bfloat16)
    local = pltpu.make_async_copy(piece, table.at[2 * c + d], local_sem)
    local.start()
    local.wait()
    ring = Ring(table, SHARE * 2 // 3, SHARE, sent_t, come_t)
    ring.hop1()
    ring.cross((0, 0))
    ring.hop2()
    ring.hop3()
    ring.hop4()
    ring.hop5()
    ring.crossed((0, 0), *Ring.set2, *Ring.set3, *Ring.set4, *Ring.set5)
    for copy in weights:
        copy.wait_send()
    ring.across(0, 0).wait_send()
    ring.drain()
    ids_copy.wait()


def token_table(shares, embed, gain, ids):
    vmem = pl.BlockSpec(memory_space=pltpu.VMEM)
    anywhere = pl.BlockSpec(memory_space=pl.ANY)
    vocab, width = embed.shape
    semaphores = [pltpu.SemaphoreType.DMA((PEERS,))] * 2 + [pltpu.SemaphoreType.DMA((36,))] * 2
    return pl.pallas_call(
        table_kernel,
        out_shape=(
            jax.ShapeDtypeStruct((2 * PEERS, SHARE, vocab), jnp.bfloat16),
            jax.ShapeDtypeStruct(ids.shape, jnp.int32),
            jax.ShapeDtypeStruct((vocab, width // SIDE), jnp.bfloat16),
        ),
        in_specs=[vmem, anywhere, vmem, anywhere],
        out_specs=(anywhere, anywhere, vmem),
        scratch_shapes=[
            pltpu.VMEM((PEERS, SHARE, DEPTH), jnp.bfloat16),
            pltpu.VMEM((vocab, width), jnp.bfloat16),
            pltpu.VMEM((PEERS, vocab, DEPTH), jnp.bfloat16),
            pltpu.VMEM((SHARE, vocab), jnp.bfloat16),
            *semaphores,
            pltpu.SemaphoreType.DMA((2,)),
            pltpu.SemaphoreType.DMA,
            pltpu.SemaphoreType.DMA,
        ],
        compiler_params=pltpu.CompilerParams(
            collective_id=0, has_side_effects=True, vmem_limit_bytes=40 * 2**20
        ),
        cost_estimate=pl.CostEstimate(flops=2 * SHARE * vocab * width, bytes_accessed=2**24, transcendentals=0),
    )(shares, embed, gain, ids)


def block_kernel(
    ids_ref,
    age_ref,
    table_in,
    short_ref,
    filt_ref,
    decay_ref,
    columns,
    weight,
    out_ref,
    table,
    onehot,
    mask1,
    mask2,
    src,
    prod,
    windows,
    recents,
    taps,
    longs,
    gates,
    total,
    weights,
    sent_own,
    come_own,
    sent_pass,
    come_pass,
    sent_w,
    come_w,
    local_sem,
):
    d = lax.axis_index("dp")
    c = lax.axis_index("context")
    t = lax.axis_index("tensor")
    right = lax.rem(t + 1, SIDE)
    left = lax.rem(t + SIDE - 1, SIDE)
    other = {"dp": 1 - d}
    local_table = pltpu.make_async_copy(table_in, table, local_sem.at[2])
    local_table.start()
    greet(
        [{"tensor": right}, {"tensor": left}, other]
        + [{"context": moved(c, k, 1)} for k in range(1, PEERS)]
    )
    local = [pltpu.make_async_copy(weight.at[h], weights.at[2 * c + h], local_sem.at[h]) for h in range(2)]
    for copy in local:
        copy.start()
    outs = Ring(weights, LANES // 2, LANES, sent_w, come_w)

    vocab = onehot.shape[1]
    ids = jnp.broadcast_to(ids_ref[...], (EXT, vocab))
    onehot[...] = jnp.where(ids == lax.broadcasted_iota(jnp.int32, (EXT, vocab), 1), 1.0, 0.0).astype(jnp.bfloat16)
    age = jnp.broadcast_to(age_ref[...], (EXT, LANES))
    mask1[...] = (age >= 1).astype(jnp.float32)
    mask2[...] = (age >= 2).astype(jnp.float32)
    src[0:8, :] = jnp.zeros((8, 3 * LANES), jnp.float32)
    for copy in local:
        copy.wait()
    outs.hop1()
    local_table.wait()

    def own_copies(i):
        return (
            send(gates.at[t, i], gates.at[t, i], sent_own.at[0, i], come_own.at[0, i], {"tensor": right}),
            send(gates.at[t, i], gates.at[t, i], sent_own.at[1, i], come_own.at[1, i], {"tensor": left}),
        )

    def pass_copies(i):
        low = (i, pl.ds(0, HALF))
        high = (i, pl.ds(HALF, HALF))
        return (
            send(gates.at[left, *low], gates.at[left, *low], sent_pass.at[0, i], come_pass.at[0, i], {"tensor": right}),
            send(gates.at[right, *high], gates.at[right, *high], sent_pass.at[1, i], come_pass.at[1, i], {"tensor": left}),
        )

    def hand_on(i):
        own, further = own_copies(i), pass_copies(i)
        for direction in range(2):
            own[direction].wait_recv()
            further[direction].start()

    def chunk(i, carry):
        for at, hop in ((1, outs.hop2), (3, outs.hop3), (5, outs.hop4), (6, outs.hop5)):
            pl.when(i == at)(hop)

        pieces = table[pl.ds(i * 4, 4)].reshape(3 * LANES, vocab)
        src[8:, :] = lax.dot_general(
            onehot[...], pieces, (((1,), (1,)), ((), ())), preferred_element_type=jnp.float32
        )
        tap_index = lax.broadcasted_iota(jnp.int32, (TAPS, LANES), 0).astype(jnp.float32)
        channels = pl.ds(pl.multiple_of(i * LANES, LANES), LANES)
        values = filt_ref[:, channels] * jnp.exp(-decay_ref[:, channels] * tap_index)
        for j in range(TAPS):
            taps[j] = jnp.broadcast_to(values[j : j + 1], (8, LANES))
        filters = short_ref[:, :, channels]

        def mixed(g, low, count):
            lanes = slice(g * LANES, (g + 1) * LANES)
            return (
                filters[0, g : g + 1] * src[pl.ds(8 + low, count), lanes]
                + filters[1, g : g + 1] * (src[pl.ds(7 + low, count), lanes] * mask1[pl.ds(low, count), :])
                + filters[2, g : g + 1] * (src[pl.ds(6 + low, count), lanes] * mask2[pl.ds(low, count), :])
            )

        for low in range(0, EXT, 48):
            product = mixed(1, low, 48) * mixed(2, low, 48)
            prod[pl.ds(low, 48), :] = product.astype(jnp.bfloat16).astype(jnp.float32)

        def piece(n, window, recent):
            row = pl.multiple_of(HALO + n * R, 16)
            head = row - jnp.broadcast_to(age_ref[pl.ds(row, 1), :], (TAPS, LANES))
            before = row - TAPS + lax.broadcasted_iota(jnp.int32, (TAPS, LANES), 0)
            window[...] = jnp.where(before >= head, prod[pl.ds(row - TAPS, TAPS), :], 0.0)
            recent[...] = prod[pl.ds(row - 8, R + 8), :]
            age = jnp.broadcast_to(age_ref[pl.ds(row, R), :], (R, LANES))
            sums = [jnp.zeros((8, LANES), jnp.float32) for _ in range(R // 8)]
            near = [jnp.zeros((8, LANES), jnp.float32) for _ in range(R // 8)]
            for phase in range(8):
                for block in range(0, TAPS // 8, GROUP):
                    held = [taps[phase + 8 * (block + m)] for m in range(GROUP)]
                    views = {
                        q: window[pl.ds(TAPS + 8 * q - phase, 8), :]
                        if q < 0
                        else recent[pl.ds(8 + 8 * q - phase, 8), :]
                        for q in range(-(block + GROUP - 1), R // 8 - block)
                    }
                    for i in range(R // 8):
                        far, close = [], []
                        for m in range(GROUP):
                            q = i - block - m
                            if q < 0:
                                far.append(held[m] * views[q])
                            else:
                                kept = age[8 * i : 8 * i + 8] >= phase + 8 * (block + m)
                                close.append(held[m] * jnp.where(kept, views[q], 0.0))
                        if far:
                            sums[i] = sums[i] + tree_sum(far)
                        if close:
                            near[i] = near[i] + tree_sum(close)
            mine = row + lax.broadcasted_iota(jnp.int32, (R, LANES), 0) - age == head[:R]
            result = jnp.where(mine, jnp.concatenate(sums, axis=0), 0.0) + jnp.concatenate(near, axis=0)
            longs[pl.ds(pl.multiple_of(n * R, R), R), :] = result

        def two_pieces(n, carry):
            for k in range(2):
                piece(2 * n + k, windows.at[k], recents.at[k])
            return carry

        lax.fori_loop(0, PIECES // 2, two_pieces, 0)
        for low in range(0, ROWS, 48):
            gated = mixed(0, HALO + low, 48) * longs[pl.ds(low, 48), :]
            gates[t, i, pl.ds(low, 48), :] = gated.astype(jnp.bfloat16)
        for copy in own_copies(i):
            copy.start()

        @pl.when(i > 0)
        def _():
            hand_on(i - 1)

        return carry

    lax.fori_loop(0, CHUNKS, chunk, 0)

    total[...] = jnp.dot(onehot[HALO:, :], columns[...], preferred_element_type=jnp.float32)
    outs.crossed(*Ring.set2, *Ring.set3, *Ring.set4, *Ring.set5)

    def finish(i, carry):
        for copy in pass_copies(i):
            copy.wait_recv()
        features = jnp.concatenate([gates[s, i] for s in range(SIDE)], axis=1)
        rows = jnp.concatenate([weights[s * CHUNKS + i] for s in range(SIDE)], axis=0)
        total[...] += jnp.dot(features, rows, preferred_element_type=jnp.float32)
        return carry

    lax.fori_loop(0, CHUNKS // 2, finish, 0)
    hand_on(CHUNKS - 1)
    lax.fori_loop(CHUNKS // 2, CHUNKS, finish, 0)
    out_ref[...] = total[...].astype(jnp.bfloat16)

    def drain(i, carry):
        for copy in own_copies(i) + pass_copies(i):
            copy.wait_send()
        return carry

    lax.fori_loop(0, CHUNKS, drain, 0)
    outs.drain()


def block_rows(ids, age, table, short_filter, mr_filter, mr_decay, columns, weight):
    vocab = table.shape[2]
    width = columns.shape[1]
    vmem = pl.BlockSpec(memory_space=pltpu.VMEM)
    anywhere = pl.BlockSpec(memory_space=pl.ANY)
    return pl.pallas_call(
        block_kernel,
        out_shape=jax.ShapeDtypeStruct((ROWS, width), jnp.bfloat16),
        in_specs=[vmem] * 2 + [anywhere] + [vmem] * 4 + [anywhere],
        out_specs=vmem,
        scratch_shapes=[
            pltpu.VMEM(table.shape, jnp.bfloat16),
            pltpu.VMEM((EXT, vocab), jnp.bfloat16),
            pltpu.VMEM((EXT, LANES), jnp.float32),
            pltpu.VMEM((EXT, LANES), jnp.float32),
            pltpu.VMEM((EXT + 8, 3 * LANES), jnp.float32),
            pltpu.VMEM((EXT, LANES), jnp.float32),
            pltpu.VMEM((2, TAPS, LANES), jnp.float32),
            pltpu.VMEM((2, R + 8, LANES), jnp.float32),
            pltpu.VMEM((TAPS, 8, LANES), jnp.float32),
            pltpu.VMEM((ROWS, LANES), jnp.float32),
            pltpu.VMEM((SIDE, CHUNKS, ROWS, LANES), jnp.bfloat16),
            pltpu.VMEM((ROWS, width), jnp.float32),
            pltpu.VMEM((2 * PEERS, DEPTH // 2, width), jnp.bfloat16),
            pltpu.SemaphoreType.DMA((2, CHUNKS)),
            pltpu.SemaphoreType.DMA((2, CHUNKS)),
            pltpu.SemaphoreType.DMA((2, CHUNKS)),
            pltpu.SemaphoreType.DMA((2, CHUNKS)),
            pltpu.SemaphoreType.DMA((36,)),
            pltpu.SemaphoreType.DMA((36,)),
            pltpu.SemaphoreType.DMA((3,)),
        ],
        compiler_params=pltpu.CompilerParams(
            collective_id=1, has_side_effects=True, vmem_limit_bytes=40 * 2**20
        ),
        cost_estimate=pl.CostEstimate(flops=2 * ROWS * width * 4096, bytes_accessed=2**24, transcendentals=0),
    )(ids, age, table, short_filter, mr_filter, mr_decay, columns, weight)


def body(
    token_ids,
    subst_pos,
    subst_base,
    window_lengths,
    embed_table,
    norm_gain,
    in_weight,
    short_filter,
    mr_filter,
    mr_decay,
    out_weight,
):
    row_count = token_ids.shape[0]
    vocab = embed_table.shape[0]
    width = out_weight.shape[1]

    matches = subst_pos[:, None] == jnp.arange(row_count, dtype=jnp.int32)[None, :]
    chosen = jnp.max(jnp.where(matches, subst_base[:, None], -1), axis=0)
    new_ids = jnp.where(chosen >= 0, chosen, token_ids)

    shares = in_weight.reshape(DEPTH, 3, CHUNKS, LANES).transpose(2, 1, 3, 0).reshape(PEERS, 2, SHARE, DEPTH)
    shares = lax.dynamic_index_in_dim(shares, lax.axis_index("dp"), 1, keepdims=False)
    table, before, columns = token_table(shares, embed_table, norm_gain[None, :], new_ids.reshape(-1, LANES))
    ids = jnp.concatenate([before.reshape(-1)[row_count - HALO :], new_ids])

    first_row = lax.axis_index("context") * row_count - HALO
    windows = jnp.arange(window_lengths.shape[0], dtype=jnp.int32)
    starts = jnp.sum(jnp.where(windows[None, :] < windows[:, None], window_lengths[None, :], 0), axis=1)
    positions = first_row + jnp.arange(EXT, dtype=jnp.int32)
    begins = jnp.max(jnp.where(starts[None, :] <= positions[:, None], starts[None, :], -1), axis=1)
    age = jnp.where(begins >= 0, positions - begins, -1)
    return block_rows(
        ids[:, None],
        age[:, None],
        table,
        short_filter,
        mr_filter,
        mr_decay[None, :],
        columns,
        out_weight.reshape(2, DEPTH // 2, width),
    )


def solution(mesh):
    in_specs = (
        P(("dp", "context")),
        P(("dp", "context")),
        P(("dp", "context")),
        P("dp"),
        P(),
        P(),
        P("context", None, "tensor"),
        P(None, None, "tensor"),
        P(None, "tensor"),
        P("tensor"),
        P("context", "tensor"),
    )
    out_specs = P(("dp", "context"), "tensor")
    return jax.shard_map(body, mesh=mesh, in_specs=in_specs, out_specs=out_specs, check_vma=False)
```

```python
import jax
import jax.numpy as jnp
from jax import lax
from jax.experimental import pallas as pl
from jax.experimental.pallas import tpu as pltpu
from jax.sharding import PartitionSpec as P

ROWS = 768
HALO = 144
EXT = HALO + ROWS
TAPS = 128
LANES = 128
R = 32
PIECES = ROWS // R
GROUP = 4
DEPTH = 256
SIDE = 4
PEERS = SIDE * SIDE
CHUNKS = 8
SHARE = 3 * LANES * CHUNKS // (2 * PEERS)
HALF = ROWS // 2
MESH = pl.DeviceIdType.MESH


def moved(c, k, sign):
    x = lax.rem(c // SIDE + SIDE + sign * (k // SIDE), SIDE)
    z = lax.rem(lax.rem(c, SIDE) + SIDE + sign * (k % SIDE), SIDE)
    return x * SIDE + z


def tree_sum(terms):
    while len(terms) > 1:
        terms = [sum(terms[k + 1 : k + 2], terms[k]) for k in range(0, len(terms), 2)]
    return terms[0]


def greet(axis_targets):
    barrier = pltpu.get_barrier_semaphore()
    for target in axis_targets:
        pl.semaphore_signal(barrier, inc=1, device_id=target, device_id_type=MESH)
    pl.semaphore_wait(barrier, len(axis_targets))


def send(source, target, sent, arrived, where):
    return pltpu.make_async_remote_copy(
        src_ref=source, dst_ref=target, send_sem=sent, recv_sem=arrived, device_id=where, device_id_type=MESH
    )


class Ring:
    def __init__(self, buffer, low, rows, sent, come):
        d = lax.axis_index("dp")
        c = lax.axis_index("context")
        self.x, self.z, self.d = c // SIDE, lax.rem(c, SIDE), d
        self.buffer, self.sent, self.come = buffer, sent, come
        self.low, self.high = pl.ds(0, low), pl.ds(low, rows - low)

    def context(self, j, m):
        dx = (1 - self.d) * m + self.d * j
        dz = (1 - self.d) * j + self.d * m
        return lax.rem(self.x + dx, SIDE) * SIDE + lax.rem(self.z + dz, SIDE)

    def copy(self, j, m, part, index, where):
        at = 2 * self.context(j, m) + self.d
        slot = self.buffer.at[at] if part is None else self.buffer.at[at, part]
        return send(slot, slot, self.sent.at[index], self.come.at[index], where)

    def along_a(self, side):
        return {"context": self.context(3 if side else 1, 0)}

    def along_b(self, side):
        return {"context": self.context(0, 3 if side else 1)}

    def first(self, side):
        return self.copy(0, 0, None, side, self.along_a(side))

    def second(self, side):
        return self.copy(1 if side else 3, 0, self.high if side else self.low, 2 + side, self.along_a(side))

    def third(self, j, side):
        return self.copy(j, 0, None, 4 + 2 * j + side, self.along_b(side))

    def fourth(self, j, side):
        return self.copy(
            j, 1 if side else 3, self.high if side else self.low, 12 + 2 * j + side, self.along_b(side)
        )

    def across(self, j, m):
        return self.copy(j, m, None, 20 + 4 * j + m, {"dp": 1 - self.d})

    def cross(self, *slots):
        for j, m in slots:
            self.across(j, m).start()

    def crossed(self, *slots):
        for j, m in slots:
            self.across(j, m).wait_recv()

    def hop1(self):
        for side in range(2):
            self.first(side).start()
            self.third(0, side).start()

    def hop2(self):
        for side in range(2):
            self.first(side).wait_recv()
            self.second(side).start()
            self.third(0, side).wait_recv()
            self.fourth(0, side).start()
        self.cross(*self.set2)
        for j in (1, 3):
            for side in range(2):
                self.third(j, side).start()

    def hop3(self):
        for side in range(2):
            self.second(side).wait_recv()
        for side in range(2):
            self.third(2, side).start()
        for side in range(2):
            self.fourth(0, side).wait_recv()
        for j in (1, 3):
            for side in range(2):
                self.third(j, side).wait_recv()
                self.fourth(j, side).start()
        self.cross(*self.set3)

    def hop4(self):
        for side in range(2):
            self.third(2, side).wait_recv()
            self.fourth(2, side).start()
        for j in (1, 3):
            for side in range(2):
                self.fourth(j, side).wait_recv()
        self.cross(*self.set4)

    def hop5(self):
        for side in range(2):
            self.fourth(2, side).wait_recv()
        self.cross(*self.set5)

    set2 = ((1, 0), (3, 0), (0, 1), (0, 3))
    set3 = ((2, 0), (0, 2), (1, 1), (1, 3), (3, 1), (3, 3))
    set4 = ((2, 1), (2, 3), (1, 2), (3, 2))
    set5 = ((2, 2),)

    def drain(self):
        for side in range(2):
            self.first(side).wait_send()
            self.second(side).wait_send()
            for j in range(SIDE):
                self.third(j, side).wait_send()
                self.fourth(j, side).wait_send()
        for j, m in self.set2 + self.set3 + self.set4 + self.set5:
            self.across(j, m).wait_send()


def table_kernel(
    shares,
    embed,
    gain,
    ids,
    table,
    before,
    columns,
    got,
    wide,
    normed,
    piece,
    sent_w,
    come_w,
    sent_t,
    come_t,
    ids_sem,
    local_sem,
    embed_sem,
):
    d = lax.axis_index("dp")
    c = lax.axis_index("context")
    local_embed = pltpu.make_async_copy(embed, wide, embed_sem)
    local_embed.start()
    other = {"dp": 1 - d}
    following = lax.rem(c + 1, PEERS)
    previous = lax.rem(c + PEERS - 1, PEERS)
    greet(
        [{"context": moved(c, k, 1)} for k in range(1, PEERS)]
        + [other, {"context": following}, {"context": previous}]
    )
    weights = [
        send(shares.at[moved(c, k, 1)], got.at[c], sent_w.at[k], come_w.at[k], {"context": moved(c, k, 1)})
        for k in range(1, PEERS)
    ]
    for copy in weights:
        copy.start()
    ids_copy = send(ids, before, ids_sem.at[0], ids_sem.at[1], {"context": following})
    ids_copy.start()

    local_embed.wait()
    vocab, width = embed.shape
    step = 32

    def norm_rows(i, carry):
        rows = pl.ds(pl.multiple_of(i * step, step), step)
        values = wide[rows, :].astype(jnp.float32)
        scale = lax.rsqrt(jnp.mean(values * values, axis=1, keepdims=True) + 1e-06)
        values = (values * scale * gain[...]).astype(jnp.bfloat16)
        for s in range(PEERS):
            normed[s, rows, :] = values[:, s * DEPTH : (s + 1) * DEPTH]
        return carry

    lax.fori_loop(0, vocab // step, norm_rows, 0)

    own = pl.ds(pl.multiple_of(lax.axis_index("tensor") * columns.shape[1], LANES), columns.shape[1])
    columns[...] = wide[:, own]

    def product(weight, s):
        return lax.dot_general(
            weight, normed[s], (((1,), (1,)), ((), ())), preferred_element_type=jnp.float32
        )

    total = product(shares[c], c)
    for k in range(1, PEERS):
        weights[k - 1].wait_recv()
        origin = moved(c, k, -1)
        total = total + product(got[origin], origin)
    piece[...] = total.astype(jnp.bfloat16)
    local = pltpu.make_async_copy(piece, table.at[2 * c + d], local_sem)
    local.start()
    local.wait()
    ring = Ring(table, SHARE * 2 // 3, SHARE, sent_t, come_t)
    ring.hop1()
    ring.cross((0, 0))
    ring.hop2()
    ring.hop3()
    ring.hop4()
    ring.hop5()
    ring.crossed((0, 0), *Ring.set2, *Ring.set3, *Ring.set4, *Ring.set5)
    for copy in weights:
        copy.wait_send()
    ring.across(0, 0).wait_send()
    ring.drain()
    ids_copy.wait()


def token_table(shares, embed, gain, ids):
    vmem = pl.BlockSpec(memory_space=pltpu.VMEM)
    anywhere = pl.BlockSpec(memory_space=pl.ANY)
    vocab, width = embed.shape
    semaphores = [pltpu.SemaphoreType.DMA((PEERS,))] * 2 + [pltpu.SemaphoreType.DMA((36,))] * 2
    return pl.pallas_call(
        table_kernel,
        out_shape=(
            jax.ShapeDtypeStruct((2 * PEERS, SHARE, vocab), jnp.bfloat16),
            jax.ShapeDtypeStruct(ids.shape, jnp.int32),
            jax.ShapeDtypeStruct((vocab, width // SIDE), jnp.bfloat16),
        ),
        in_specs=[vmem, anywhere, vmem, anywhere],
        out_specs=(anywhere, anywhere, vmem),
        scratch_shapes=[
            pltpu.VMEM((PEERS, SHARE, DEPTH), jnp.bfloat16),
            pltpu.VMEM((vocab, width), jnp.bfloat16),
            pltpu.VMEM((PEERS, vocab, DEPTH), jnp.bfloat16),
            pltpu.VMEM((SHARE, vocab), jnp.bfloat16),
            *semaphores,
            pltpu.SemaphoreType.DMA((2,)),
            pltpu.SemaphoreType.DMA,
            pltpu.SemaphoreType.DMA,
        ],
        compiler_params=pltpu.CompilerParams(
            collective_id=0, has_side_effects=True, vmem_limit_bytes=40 * 2**20
        ),
        cost_estimate=pl.CostEstimate(flops=2 * SHARE * vocab * width, bytes_accessed=2**24, transcendentals=0),
    )(shares, embed, gain, ids)


def block_kernel(
    ids_ref,
    age_ref,
    table_in,
    short_ref,
    filt_ref,
    decay_ref,
    columns,
    weight,
    out_ref,
    table,
    onehot,
    mask1,
    mask2,
    src,
    prod,
    windows,
    recents,
    taps,
    longs,
    gates,
    total,
    weights,
    sent_own,
    come_own,
    sent_pass,
    come_pass,
    sent_w,
    come_w,
    local_sem,
):
    d = lax.axis_index("dp")
    c = lax.axis_index("context")
    t = lax.axis_index("tensor")
    right = lax.rem(t + 1, SIDE)
    left = lax.rem(t + SIDE - 1, SIDE)
    other = {"dp": 1 - d}
    local_table = pltpu.make_async_copy(table_in, table, local_sem.at[2])
    local_table.start()
    greet(
        [{"tensor": right}, {"tensor": left}, other]
        + [{"context": moved(c, k, 1)} for k in range(1, PEERS)]
    )
    local = [pltpu.make_async_copy(weight.at[h], weights.at[2 * c + h], local_sem.at[h]) for h in range(2)]
    for copy in local:
        copy.start()
    outs = Ring(weights, LANES // 2, LANES, sent_w, come_w)

    vocab = onehot.shape[1]
    ids = jnp.broadcast_to(ids_ref[...], (EXT, vocab))
    onehot[...] = jnp.where(ids == lax.broadcasted_iota(jnp.int32, (EXT, vocab), 1), 1.0, 0.0).astype(jnp.bfloat16)
    age = jnp.broadcast_to(age_ref[...], (EXT, LANES))
    mask1[...] = (age >= 1).astype(jnp.float32)
    mask2[...] = (age >= 2).astype(jnp.float32)
    src[0:8, :] = jnp.zeros((8, 3 * LANES), jnp.float32)
    for copy in local:
        copy.wait()
    outs.hop1()
    local_table.wait()

    def own_copies(i):
        return (
            send(gates.at[t, i], gates.at[t, i], sent_own.at[0, i], come_own.at[0, i], {"tensor": right}),
            send(gates.at[t, i], gates.at[t, i], sent_own.at[1, i], come_own.at[1, i], {"tensor": left}),
        )

    def pass_copies(i):
        low = (i, pl.ds(0, HALF))
        high = (i, pl.ds(HALF, HALF))
        return (
            send(gates.at[left, *low], gates.at[left, *low], sent_pass.at[0, i], come_pass.at[0, i], {"tensor": right}),
            send(gates.at[right, *high], gates.at[right, *high], sent_pass.at[1, i], come_pass.at[1, i], {"tensor": left}),
        )

    def hand_on(i):
        own, further = own_copies(i), pass_copies(i)
        for direction in range(2):
            own[direction].wait_recv()
            further[direction].start()

    def chunk(i, carry):
        for at, hop in ((1, outs.hop2), (3, outs.hop3), (5, outs.hop4), (6, outs.hop5)):
            pl.when(i == at)(hop)

        pieces = table[pl.ds(i * 4, 4)].reshape(3 * LANES, vocab)
        src[8:, :] = lax.dot_general(
            onehot[...], pieces, (((1,), (1,)), ((), ())), preferred_element_type=jnp.float32
        )
        tap_index = lax.broadcasted_iota(jnp.int32, (TAPS, LANES), 0).astype(jnp.float32)
        channels = pl.ds(pl.multiple_of(i * LANES, LANES), LANES)
        values = filt_ref[:, channels] * jnp.exp(-decay_ref[:, channels] * tap_index)
        for j in range(TAPS):
            taps[j] = jnp.broadcast_to(values[j : j + 1], (8, LANES))
        filters = short_ref[:, :, channels]

        def mixed(g, low, count):
            lanes = slice(g * LANES, (g + 1) * LANES)
            return (
                filters[0, g : g + 1] * src[pl.ds(8 + low, count), lanes]
                + filters[1, g : g + 1] * (src[pl.ds(7 + low, count), lanes] * mask1[pl.ds(low, count), :])
                + filters[2, g : g + 1] * (src[pl.ds(6 + low, count), lanes] * mask2[pl.ds(low, count), :])
            )

        for low in range(0, EXT, 48):
            product = mixed(1, low, 48) * mixed(2, low, 48)
            prod[pl.ds(low, 48), :] = product.astype(jnp.bfloat16).astype(jnp.float32)

        def piece(n, window, recent):
            row = pl.multiple_of(HALO + n * R, 16)
            head = row - jnp.broadcast_to(age_ref[pl.ds(row, 1), :], (TAPS, LANES))
            before = row - TAPS + lax.broadcasted_iota(jnp.int32, (TAPS, LANES), 0)
            window[...] = jnp.where(before >= head, prod[pl.ds(row - TAPS, TAPS), :], 0.0)
            recent[...] = prod[pl.ds(row - 8, R + 8), :]
            age = jnp.broadcast_to(age_ref[pl.ds(row, R), :], (R, LANES))
            sums = [jnp.zeros((8, LANES), jnp.float32) for _ in range(R // 8)]
            near = [jnp.zeros((8, LANES), jnp.float32) for _ in range(R // 8)]
            for phase in range(8):
                for block in range(0, TAPS // 8, GROUP):
                    held = [taps[phase + 8 * (block + m)] for m in range(GROUP)]
                    views = {
                        q: window[pl.ds(TAPS + 8 * q - phase, 8), :]
                        if q < 0
                        else recent[pl.ds(8 + 8 * q - phase, 8), :]
                        for q in range(-(block + GROUP - 1), R // 8 - block)
                    }
                    for i in range(R // 8):
                        far, close = [], []
                        for m in range(GROUP):
                            q = i - block - m
                            if q < 0:
                                far.append(held[m] * views[q])
                            else:
                                tap = phase + 8 * (block + m)
                                kept = age[8 * i : 8 * i + 8] >= tap
                                close.append(held[m] * (jnp.where(kept, views[q], 0.0) if tap else views[q]))
                        if far:
                            sums[i] = sums[i] + tree_sum(far)
                        if close:
                            near[i] = near[i] + tree_sum(close)
            mine = row + lax.broadcasted_iota(jnp.int32, (R, LANES), 0) - age == head[:R]
            result = jnp.where(mine, jnp.concatenate(sums, axis=0), 0.0) + jnp.concatenate(near, axis=0)
            longs[pl.ds(pl.multiple_of(n * R, R), R), :] = result

        def two_pieces(n, carry):
            @pl.when((i > 0) & (n == PIECES // 4))
            def _():
                hand_on(i - 1)

            for k in range(2):
                piece(2 * n + k, windows.at[k], recents.at[k])
            return carry

        lax.fori_loop(0, PIECES // 2, two_pieces, 0)
        for low in range(0, ROWS, 48):
            gated = mixed(0, HALO + low, 48) * longs[pl.ds(low, 48), :]
            gates[t, i, pl.ds(low, 48), :] = gated.astype(jnp.bfloat16)
        for copy in own_copies(i):
            copy.start()

        return carry

    lax.fori_loop(0, CHUNKS, chunk, 0)

    total[...] = jnp.dot(onehot[HALO:, :], columns[...], preferred_element_type=jnp.float32)
    outs.crossed(*Ring.set2, *Ring.set3, *Ring.set4, *Ring.set5)

    def finish(i, carry):
        for copy in pass_copies(i):
            copy.wait_recv()
        features = jnp.concatenate([gates[s, i] for s in range(SIDE)], axis=1)
        rows = jnp.concatenate([weights[s * CHUNKS + i] for s in range(SIDE)], axis=0)
        total[...] += jnp.dot(features, rows, preferred_element_type=jnp.float32)
        return carry

    lax.fori_loop(0, CHUNKS // 2, finish, 0)
    hand_on(CHUNKS - 1)
    lax.fori_loop(CHUNKS // 2, CHUNKS, finish, 0)
    out_ref[...] = total[...].astype(jnp.bfloat16)

    def drain(i, carry):
        for copy in own_copies(i) + pass_copies(i):
            copy.wait_send()
        return carry

    lax.fori_loop(0, CHUNKS, drain, 0)
    outs.drain()


def block_rows(ids, age, table, short_filter, mr_filter, mr_decay, columns, weight):
    vocab = table.shape[2]
    width = columns.shape[1]
    vmem = pl.BlockSpec(memory_space=pltpu.VMEM)
    anywhere = pl.BlockSpec(memory_space=pl.ANY)
    return pl.pallas_call(
        block_kernel,
        out_shape=jax.ShapeDtypeStruct((ROWS, width), jnp.bfloat16),
        in_specs=[vmem] * 2 + [anywhere] + [vmem] * 4 + [anywhere],
        out_specs=vmem,
        scratch_shapes=[
            pltpu.VMEM(table.shape, jnp.bfloat16),
            pltpu.VMEM((EXT, vocab), jnp.bfloat16),
            pltpu.VMEM((EXT, LANES), jnp.float32),
            pltpu.VMEM((EXT, LANES), jnp.float32),
            pltpu.VMEM((EXT + 8, 3 * LANES), jnp.float32),
            pltpu.VMEM((EXT, LANES), jnp.float32),
            pltpu.VMEM((2, TAPS, LANES), jnp.float32),
            pltpu.VMEM((2, R + 8, LANES), jnp.float32),
            pltpu.VMEM((TAPS, 8, LANES), jnp.float32),
            pltpu.VMEM((ROWS, LANES), jnp.float32),
            pltpu.VMEM((SIDE, CHUNKS, ROWS, LANES), jnp.bfloat16),
            pltpu.VMEM((ROWS, width), jnp.float32),
            pltpu.VMEM((2 * PEERS, DEPTH // 2, width), jnp.bfloat16),
            pltpu.SemaphoreType.DMA((2, CHUNKS)),
            pltpu.SemaphoreType.DMA((2, CHUNKS)),
            pltpu.SemaphoreType.DMA((2, CHUNKS)),
            pltpu.SemaphoreType.DMA((2, CHUNKS)),
            pltpu.SemaphoreType.DMA((36,)),
            pltpu.SemaphoreType.DMA((36,)),
            pltpu.SemaphoreType.DMA((3,)),
        ],
        compiler_params=pltpu.CompilerParams(
            collective_id=1, has_side_effects=True, vmem_limit_bytes=40 * 2**20
        ),
        cost_estimate=pl.CostEstimate(flops=2 * ROWS * width * 4096, bytes_accessed=2**24, transcendentals=0),
    )(ids, age, table, short_filter, mr_filter, mr_decay, columns, weight)


def body(
    token_ids,
    subst_pos,
    subst_base,
    window_lengths,
    embed_table,
    norm_gain,
    in_weight,
    short_filter,
    mr_filter,
    mr_decay,
    out_weight,
):
    row_count = token_ids.shape[0]
    vocab = embed_table.shape[0]
    width = out_weight.shape[1]

    matches = subst_pos[:, None] == jnp.arange(row_count, dtype=jnp.int32)[None, :]
    chosen = jnp.max(jnp.where(matches, subst_base[:, None], -1), axis=0)
    new_ids = jnp.where(chosen >= 0, chosen, token_ids)

    shares = in_weight.reshape(DEPTH, 3, CHUNKS, LANES).transpose(2, 1, 3, 0).reshape(PEERS, 2, SHARE, DEPTH)
    shares = lax.dynamic_index_in_dim(shares, lax.axis_index("dp"), 1, keepdims=False)
    table, before, columns = token_table(shares, embed_table, norm_gain[None, :], new_ids.reshape(-1, LANES))
    ids = jnp.concatenate([before.reshape(-1)[row_count - HALO :], new_ids])

    first_row = lax.axis_index("context") * row_count - HALO
    windows = jnp.arange(window_lengths.shape[0], dtype=jnp.int32)
    starts = jnp.sum(jnp.where(windows[None, :] < windows[:, None], window_lengths[None, :], 0), axis=1)
    positions = first_row + jnp.arange(EXT, dtype=jnp.int32)
    begins = jnp.max(jnp.where(starts[None, :] <= positions[:, None], starts[None, :], -1), axis=1)
    age = jnp.where(begins >= 0, positions - begins, -1)
    return block_rows(
        ids[:, None],
        age[:, None],
        table,
        short_filter,
        mr_filter,
        mr_decay[None, :],
        columns,
        out_weight.reshape(2, DEPTH // 2, width),
    )


def solution(mesh):
    in_specs = (
        P(("dp", "context")),
        P(("dp", "context")),
        P(("dp", "context")),
        P("dp"),
        P(),
        P(),
        P("context", None, "tensor"),
        P(None, None, "tensor"),
        P(None, "tensor"),
        P("tensor"),
        P("context", "tensor"),
    )
    out_specs = P(("dp", "context"), "tensor")
    return jax.shard_map(body, mesh=mesh, in_specs=in_specs, out_specs=out_specs, check_vma=False)
```

```python
import jax
import jax.numpy as jnp
from jax import lax
from jax.experimental import pallas as pl
from jax.experimental.pallas import tpu as pltpu
from jax.sharding import PartitionSpec as P

ROWS = 768
HALO = 144
EXT = HALO + ROWS
TAPS = 128
LANES = 128
R = 32
PIECES = ROWS // R
GROUP = 4
DEPTH = 256
SIDE = 4
PEERS = SIDE * SIDE
CHUNKS = 8
SHARE = 3 * LANES * CHUNKS // (2 * PEERS)
HALF = ROWS // 2
MESH = pl.DeviceIdType.MESH


def moved(c, k, sign):
    x = lax.rem(c // SIDE + SIDE + sign * (k // SIDE), SIDE)
    z = lax.rem(lax.rem(c, SIDE) + SIDE + sign * (k % SIDE), SIDE)
    return x * SIDE + z


def tree_sum(terms):
    while len(terms) > 1:
        terms = [sum(terms[k + 1 : k + 2], terms[k]) for k in range(0, len(terms), 2)]
    return terms[0]


def greet(axis_targets):
    barrier = pltpu.get_barrier_semaphore()
    for target in axis_targets:
        pl.semaphore_signal(barrier, inc=1, device_id=target, device_id_type=MESH)
    pl.semaphore_wait(barrier, len(axis_targets))


def send(source, target, sent, arrived, where):
    return pltpu.make_async_remote_copy(
        src_ref=source, dst_ref=target, send_sem=sent, recv_sem=arrived, device_id=where, device_id_type=MESH
    )


class Ring:
    def __init__(self, buffer, low, rows, sent, come):
        d = lax.axis_index("dp")
        c = lax.axis_index("context")
        self.x, self.z, self.d = c // SIDE, lax.rem(c, SIDE), d
        self.buffer, self.sent, self.come = buffer, sent, come
        self.low, self.high = pl.ds(0, low), pl.ds(low, rows - low)

    def context(self, j, m):
        dx = (1 - self.d) * m + self.d * j
        dz = (1 - self.d) * j + self.d * m
        return lax.rem(self.x + dx, SIDE) * SIDE + lax.rem(self.z + dz, SIDE)

    def copy(self, j, m, part, index, where):
        at = 2 * self.context(j, m) + self.d
        slot = self.buffer.at[at] if part is None else self.buffer.at[at, part]
        return send(slot, slot, self.sent.at[index], self.come.at[index], where)

    def along_a(self, side):
        return {"context": self.context(3 if side else 1, 0)}

    def along_b(self, side):
        return {"context": self.context(0, 3 if side else 1)}

    def first(self, side):
        return self.copy(0, 0, None, side, self.along_a(side))

    def second(self, side):
        return self.copy(1 if side else 3, 0, self.high if side else self.low, 2 + side, self.along_a(side))

    def third(self, j, side):
        return self.copy(j, 0, None, 4 + 2 * j + side, self.along_b(side))

    def fourth(self, j, side):
        return self.copy(
            j, 1 if side else 3, self.high if side else self.low, 12 + 2 * j + side, self.along_b(side)
        )

    def across(self, j, m):
        return self.copy(j, m, None, 20 + 4 * j + m, {"dp": 1 - self.d})

    def cross(self, *slots):
        for j, m in slots:
            self.across(j, m).start()

    def crossed(self, *slots):
        for j, m in slots:
            self.across(j, m).wait_recv()

    def hop1(self):
        for side in range(2):
            self.first(side).start()
            self.third(0, side).start()

    def hop2(self):
        for side in range(2):
            self.first(side).wait_recv()
            self.second(side).start()
            self.third(0, side).wait_recv()
            self.fourth(0, side).start()
        self.cross(*self.set2)
        for j in (1, 3):
            for side in range(2):
                self.third(j, side).start()

    def hop3(self):
        for side in range(2):
            self.second(side).wait_recv()
        for side in range(2):
            self.third(2, side).start()
        for side in range(2):
            self.fourth(0, side).wait_recv()
        for j in (1, 3):
            for side in range(2):
                self.third(j, side).wait_recv()
                self.fourth(j, side).start()
        self.cross(*self.set3)

    def hop4(self):
        for side in range(2):
            self.third(2, side).wait_recv()
            self.fourth(2, side).start()
        for j in (1, 3):
            for side in range(2):
                self.fourth(j, side).wait_recv()
        self.cross(*self.set4)

    def hop5(self):
        for side in range(2):
            self.fourth(2, side).wait_recv()
        self.cross(*self.set5)

    set2 = ((1, 0), (3, 0), (0, 1), (0, 3))
    set3 = ((2, 0), (0, 2), (1, 1), (1, 3), (3, 1), (3, 3))
    set4 = ((2, 1), (2, 3), (1, 2), (3, 2))
    set5 = ((2, 2),)

    def drain(self):
        for side in range(2):
            self.first(side).wait_send()
            self.second(side).wait_send()
            for j in range(SIDE):
                self.third(j, side).wait_send()
                self.fourth(j, side).wait_send()
        for j, m in self.set2 + self.set3 + self.set4 + self.set5:
            self.across(j, m).wait_send()


def table_kernel(
    shares,
    embed,
    gain,
    ids,
    table,
    before,
    columns,
    got,
    wide,
    normed,
    piece,
    sent_w,
    come_w,
    sent_t,
    come_t,
    ids_sem,
    local_sem,
    embed_sem,
):
    d = lax.axis_index("dp")
    c = lax.axis_index("context")
    local_embed = pltpu.make_async_copy(embed, wide, embed_sem)
    local_embed.start()
    other = {"dp": 1 - d}
    following = lax.rem(c + 1, PEERS)
    previous = lax.rem(c + PEERS - 1, PEERS)
    greet(
        [{"context": moved(c, k, 1)} for k in range(1, PEERS)]
        + [other, {"context": following}, {"context": previous}]
    )
    weights = [
        send(shares.at[moved(c, k, 1)], got.at[c], sent_w.at[k], come_w.at[k], {"context": moved(c, k, 1)})
        for k in range(1, PEERS)
    ]
    for copy in weights:
        copy.start()
    ids_copy = send(ids, before, ids_sem.at[0], ids_sem.at[1], {"context": following})
    ids_copy.start()

    local_embed.wait()
    vocab, width = embed.shape
    step = 32

    def norm_rows(i, carry):
        rows = pl.ds(pl.multiple_of(i * step, step), step)
        values = wide[rows, :].astype(jnp.float32)
        scale = lax.rsqrt(jnp.mean(values * values, axis=1, keepdims=True) + 1e-06)
        values = (values * scale * gain[...]).astype(jnp.bfloat16)
        for s in range(PEERS):
            normed[s, rows, :] = values[:, s * DEPTH : (s + 1) * DEPTH]
        return carry

    lax.fori_loop(0, vocab // step, norm_rows, 0)

    own = pl.ds(pl.multiple_of(lax.axis_index("tensor") * columns.shape[1], LANES), columns.shape[1])
    columns[...] = wide[:, own]

    def product(weight, s):
        return lax.dot_general(
            weight, normed[s], (((1,), (1,)), ((), ())), preferred_element_type=jnp.float32
        )

    total = product(shares[c], c)
    for k in range(1, PEERS):
        weights[k - 1].wait_recv()
        origin = moved(c, k, -1)
        total = total + product(got[origin], origin)
    piece[...] = total.astype(jnp.bfloat16)
    local = pltpu.make_async_copy(piece, table.at[2 * c + d], local_sem)
    local.start()
    local.wait()
    ring = Ring(table, SHARE * 2 // 3, SHARE, sent_t, come_t)
    ring.hop1()
    ring.cross((0, 0))
    ring.hop2()
    ring.hop3()
    ring.hop4()
    ring.hop5()
    ring.crossed((0, 0), *Ring.set2, *Ring.set3, *Ring.set4, *Ring.set5)
    for copy in weights:
        copy.wait_send()
    ring.across(0, 0).wait_send()
    ring.drain()
    ids_copy.wait()


def token_table(shares, embed, gain, ids):
    vmem = pl.BlockSpec(memory_space=pltpu.VMEM)
    anywhere = pl.BlockSpec(memory_space=pl.ANY)
    vocab, width = embed.shape
    semaphores = [pltpu.SemaphoreType.DMA((PEERS,))] * 2 + [pltpu.SemaphoreType.DMA((36,))] * 2
    return pl.pallas_call(
        table_kernel,
        out_shape=(
            jax.ShapeDtypeStruct((2 * PEERS, SHARE, vocab), jnp.bfloat16),
            jax.ShapeDtypeStruct(ids.shape, jnp.int32),
            jax.ShapeDtypeStruct((vocab, width // SIDE), jnp.bfloat16),
        ),
        in_specs=[vmem, anywhere, vmem, anywhere],
        out_specs=(anywhere, anywhere, vmem),
        scratch_shapes=[
            pltpu.VMEM((PEERS, SHARE, DEPTH), jnp.bfloat16),
            pltpu.VMEM((vocab, width), jnp.bfloat16),
            pltpu.VMEM((PEERS, vocab, DEPTH), jnp.bfloat16),
            pltpu.VMEM((SHARE, vocab), jnp.bfloat16),
            *semaphores,
            pltpu.SemaphoreType.DMA((2,)),
            pltpu.SemaphoreType.DMA,
            pltpu.SemaphoreType.DMA,
        ],
        compiler_params=pltpu.CompilerParams(
            collective_id=0, has_side_effects=True, vmem_limit_bytes=40 * 2**20
        ),
        cost_estimate=pl.CostEstimate(flops=2 * SHARE * vocab * width, bytes_accessed=2**24, transcendentals=0),
    )(shares, embed, gain, ids)


def block_kernel(
    ids_ref,
    age_ref,
    table_in,
    short_ref,
    filt_ref,
    decay_ref,
    columns,
    weight,
    out_ref,
    table,
    onehot,
    mask1,
    mask2,
    src,
    prod,
    windows,
    recents,
    taps,
    longs,
    gates,
    total,
    weights,
    sent_own,
    come_own,
    sent_pass,
    come_pass,
    sent_w,
    come_w,
    local_sem,
):
    d = lax.axis_index("dp")
    c = lax.axis_index("context")
    t = lax.axis_index("tensor")
    right = lax.rem(t + 1, SIDE)
    left = lax.rem(t + SIDE - 1, SIDE)
    other = {"dp": 1 - d}
    local_table = pltpu.make_async_copy(table_in, table, local_sem.at[2])
    local_table.start()
    greet(
        [{"tensor": right}, {"tensor": left}, other]
        + [{"context": moved(c, k, 1)} for k in range(1, PEERS)]
    )
    local = [pltpu.make_async_copy(weight.at[h], weights.at[2 * c + h], local_sem.at[h]) for h in range(2)]
    for copy in local:
        copy.start()
    outs = Ring(weights, LANES // 2, LANES, sent_w, come_w)

    vocab = onehot.shape[1]
    ids = jnp.broadcast_to(ids_ref[...], (EXT, vocab))
    onehot[...] = jnp.where(ids == lax.broadcasted_iota(jnp.int32, (EXT, vocab), 1), 1.0, 0.0).astype(jnp.bfloat16)
    age = jnp.broadcast_to(age_ref[...], (EXT, LANES))
    mask1[...] = (age >= 1).astype(jnp.float32)
    mask2[...] = (age >= 2).astype(jnp.float32)
    src[0:8, :] = jnp.zeros((8, 3 * LANES), jnp.float32)
    for copy in local:
        copy.wait()
    outs.hop1()
    local_table.wait()

    def own_copies(i):
        return (
            send(gates.at[t, i], gates.at[t, i], sent_own.at[0, i], come_own.at[0, i], {"tensor": right}),
            send(gates.at[t, i], gates.at[t, i], sent_own.at[1, i], come_own.at[1, i], {"tensor": left}),
        )

    def pass_copies(i):
        low = (i, pl.ds(0, HALF))
        high = (i, pl.ds(HALF, HALF))
        return (
            send(gates.at[left, *low], gates.at[left, *low], sent_pass.at[0, i], come_pass.at[0, i], {"tensor": right}),
            send(gates.at[right, *high], gates.at[right, *high], sent_pass.at[1, i], come_pass.at[1, i], {"tensor": left}),
        )

    def hand_on(i):
        own, further = own_copies(i), pass_copies(i)
        for direction in range(2):
            own[direction].wait_recv()
            further[direction].start()

    def chunk(i, carry):
        for at, hop in ((2, outs.hop2), (4, outs.hop3), (6, outs.hop4), (7, outs.hop5)):
            pl.when(i == at)(hop)

        pieces = table[pl.ds(i * 4, 4)].reshape(3 * LANES, vocab)
        src[8:, :] = lax.dot_general(
            onehot[...], pieces, (((1,), (1,)), ((), ())), preferred_element_type=jnp.float32
        )
        tap_index = lax.broadcasted_iota(jnp.int32, (TAPS, LANES), 0).astype(jnp.float32)
        channels = pl.ds(pl.multiple_of(i * LANES, LANES), LANES)
        values = filt_ref[:, channels] * jnp.exp(-decay_ref[:, channels] * tap_index)
        for j in range(TAPS):
            taps[j] = jnp.broadcast_to(values[j : j + 1], (8, LANES))
        filters = short_ref[:, :, channels]

        def mixed(g, low, count):
            lanes = slice(g * LANES, (g + 1) * LANES)
            return (
                filters[0, g : g + 1] * src[pl.ds(8 + low, count), lanes]
                + filters[1, g : g + 1] * (src[pl.ds(7 + low, count), lanes] * mask1[pl.ds(low, count), :])
                + filters[2, g : g + 1] * (src[pl.ds(6 + low, count), lanes] * mask2[pl.ds(low, count), :])
            )

        for low in range(0, EXT, 48):
            product = mixed(1, low, 48) * mixed(2, low, 48)
            prod[pl.ds(low, 48), :] = product.astype(jnp.bfloat16).astype(jnp.float32)

        def piece(n, window, recent):
            row = pl.multiple_of(HALO + n * R, 16)
            head = row - jnp.broadcast_to(age_ref[pl.ds(row, 1), :], (TAPS, LANES))
            before = row - TAPS + lax.broadcasted_iota(jnp.int32, (TAPS, LANES), 0)
            window[...] = jnp.where(before >= head, prod[pl.ds(row - TAPS, TAPS), :], 0.0)
            recent[...] = prod[pl.ds(row - 8, R + 8), :]
            age = jnp.broadcast_to(age_ref[pl.ds(row, R), :], (R, LANES))
            sums = [jnp.zeros((8, LANES), jnp.float32) for _ in range(R // 8)]
            near = [jnp.zeros((8, LANES), jnp.float32) for _ in range(R // 8)]
            for phase in range(8):
                for block in range(0, TAPS // 8, GROUP):
                    held = [taps[phase + 8 * (block + m)] for m in range(GROUP)]
                    views = {
                        q: window[pl.ds(TAPS + 8 * q - phase, 8), :]
                        if q < 0
                        else recent[pl.ds(8 + 8 * q - phase, 8), :]
                        for q in range(-(block + GROUP - 1), R // 8 - block)
                    }
                    for i in range(R // 8):
                        far, close = [], []
                        for m in range(GROUP):
                            q = i - block - m
                            if q < 0:
                                far.append(held[m] * views[q])
                            else:
                                kept = age[8 * i : 8 * i + 8] >= phase + 8 * (block + m)
                                close.append(held[m] * jnp.where(kept, views[q], 0.0))
                        if far:
                            sums[i] = sums[i] + tree_sum(far)
                        if close:
                            near[i] = near[i] + tree_sum(close)
            mine = row + lax.broadcasted_iota(jnp.int32, (R, LANES), 0) - age == head[:R]
            result = jnp.where(mine, jnp.concatenate(sums, axis=0), 0.0) + jnp.concatenate(near, axis=0)
            longs[pl.ds(pl.multiple_of(n * R, R), R), :] = result

        def two_pieces(n, carry):
            for k in range(2):
                piece(2 * n + k, windows.at[k], recents.at[k])
            return carry

        lax.fori_loop(0, PIECES // 2, two_pieces, 0)
        for low in range(0, ROWS, 48):
            gated = mixed(0, HALO + low, 48) * longs[pl.ds(low, 48), :]
            gates[t, i, pl.ds(low, 48), :] = gated.astype(jnp.bfloat16)
        for copy in own_copies(i):
            copy.start()

        @pl.when(i > 0)
        def _():
            hand_on(i - 1)

        return carry

    lax.fori_loop(0, CHUNKS, chunk, 0)

    total[...] = jnp.dot(onehot[HALO:, :], columns[...], preferred_element_type=jnp.float32)
    outs.crossed(*Ring.set2, *Ring.set3, *Ring.set4, *Ring.set5)

    def finish(i, carry):
        for copy in pass_copies(i):
            copy.wait_recv()
        features = jnp.concatenate([gates[s, i] for s in range(SIDE)], axis=1)
        rows = jnp.concatenate([weights[s * CHUNKS + i] for s in range(SIDE)], axis=0)
        total[...] += jnp.dot(features, rows, preferred_element_type=jnp.float32)
        return carry

    lax.fori_loop(0, CHUNKS // 2, finish, 0)
    hand_on(CHUNKS - 1)
    lax.fori_loop(CHUNKS // 2, CHUNKS, finish, 0)
    out_ref[...] = total[...].astype(jnp.bfloat16)

    def drain(i, carry):
        for copy in own_copies(i) + pass_copies(i):
            copy.wait_send()
        return carry

    lax.fori_loop(0, CHUNKS, drain, 0)
    outs.drain()


def block_rows(ids, age, table, short_filter, mr_filter, mr_decay, columns, weight):
    vocab = table.shape[2]
    width = columns.shape[1]
    vmem = pl.BlockSpec(memory_space=pltpu.VMEM)
    anywhere = pl.BlockSpec(memory_space=pl.ANY)
    return pl.pallas_call(
        block_kernel,
        out_shape=jax.ShapeDtypeStruct((ROWS, width), jnp.bfloat16),
        in_specs=[vmem] * 2 + [anywhere] + [vmem] * 4 + [anywhere],
        out_specs=vmem,
        scratch_shapes=[
            pltpu.VMEM(table.shape, jnp.bfloat16),
            pltpu.VMEM((EXT, vocab), jnp.bfloat16),
            pltpu.VMEM((EXT, LANES), jnp.float32),
            pltpu.VMEM((EXT, LANES), jnp.float32),
            pltpu.VMEM((EXT + 8, 3 * LANES), jnp.float32),
            pltpu.VMEM((EXT, LANES), jnp.float32),
            pltpu.VMEM((2, TAPS, LANES), jnp.float32),
            pltpu.VMEM((2, R + 8, LANES), jnp.float32),
            pltpu.VMEM((TAPS, 8, LANES), jnp.float32),
            pltpu.VMEM((ROWS, LANES), jnp.float32),
            pltpu.VMEM((SIDE, CHUNKS, ROWS, LANES), jnp.bfloat16),
            pltpu.VMEM((ROWS, width), jnp.float32),
            pltpu.VMEM((2 * PEERS, DEPTH // 2, width), jnp.bfloat16),
            pltpu.SemaphoreType.DMA((2, CHUNKS)),
            pltpu.SemaphoreType.DMA((2, CHUNKS)),
            pltpu.SemaphoreType.DMA((2, CHUNKS)),
            pltpu.SemaphoreType.DMA((2, CHUNKS)),
            pltpu.SemaphoreType.DMA((36,)),
            pltpu.SemaphoreType.DMA((36,)),
            pltpu.SemaphoreType.DMA((3,)),
        ],
        compiler_params=pltpu.CompilerParams(
            collective_id=1, has_side_effects=True, vmem_limit_bytes=40 * 2**20
        ),
        cost_estimate=pl.CostEstimate(flops=2 * ROWS * width * 4096, bytes_accessed=2**24, transcendentals=0),
    )(ids, age, table, short_filter, mr_filter, mr_decay, columns, weight)


def body(
    token_ids,
    subst_pos,
    subst_base,
    window_lengths,
    embed_table,
    norm_gain,
    in_weight,
    short_filter,
    mr_filter,
    mr_decay,
    out_weight,
):
    row_count = token_ids.shape[0]
    vocab = embed_table.shape[0]
    width = out_weight.shape[1]

    matches = subst_pos[:, None] == jnp.arange(row_count, dtype=jnp.int32)[None, :]
    chosen = jnp.max(jnp.where(matches, subst_base[:, None], -1), axis=0)
    new_ids = jnp.where(chosen >= 0, chosen, token_ids)

    shares = in_weight.reshape(DEPTH, 3, CHUNKS, LANES).transpose(2, 1, 3, 0).reshape(PEERS, 2, SHARE, DEPTH)
    shares = lax.dynamic_index_in_dim(shares, lax.axis_index("dp"), 1, keepdims=False)
    table, before, columns = token_table(shares, embed_table, norm_gain[None, :], new_ids.reshape(-1, LANES))
    ids = jnp.concatenate([before.reshape(-1)[row_count - HALO :], new_ids])

    first_row = lax.axis_index("context") * row_count - HALO
    windows = jnp.arange(window_lengths.shape[0], dtype=jnp.int32)
    starts = jnp.sum(jnp.where(windows[None, :] < windows[:, None], window_lengths[None, :], 0), axis=1)
    positions = first_row + jnp.arange(EXT, dtype=jnp.int32)
    begins = jnp.max(jnp.where(starts[None, :] <= positions[:, None], starts[None, :], -1), axis=1)
    age = jnp.where(begins >= 0, positions - begins, -1)
    return block_rows(
        ids[:, None],
        age[:, None],
        table,
        short_filter,
        mr_filter,
        mr_decay[None, :],
        columns,
        out_weight.reshape(2, DEPTH // 2, width),
    )


def solution(mesh):
    in_specs = (
        P(("dp", "context")),
        P(("dp", "context")),
        P(("dp", "context")),
        P("dp"),
        P(),
        P(),
        P("context", None, "tensor"),
        P(None, None, "tensor"),
        P(None, "tensor"),
        P("tensor"),
        P("context", "tensor"),
    )
    out_specs = P(("dp", "context"), "tensor")
    return jax.shard_map(body, mesh=mesh, in_specs=in_specs, out_specs=out_specs, check_vma=False)
```
